256 devices in a mesh: dp: 16 (over z, core), expert: 16 (over y, x).
Axes of the slice: x: 4, y: 4, z: 8, core: 2. Of those that a mesh axis runs over, the one named last changes fastest.
Arguments:
- tokens: bfloat16 [196608, 2048], P(('dp', 'expert')), may hold values from -6 to 6
- target: bfloat16 [196608, 2048], P(('dp', 'expert')), may hold values from -4 to 4
- route_index: int32 [16, 16, 16, 16], P('dp', None, 'expert'), may hold values from 0 to 767, as said below
- route_count: int32 [16, 16, 16], P('dp', None, 'expert'), may hold values from 1 to 16, as said below
- route_gate: float32 [16, 16, 16, 16], P('dp', None, 'expert'), may hold values from 0.1 to 1
- gate_weight: bfloat16 [2048, 16, 768], P('dp', 'expert'), may hold values from -0.125 to 0.125
- up_weight: bfloat16 [2048, 16, 768], P('dp', 'expert'), may hold values from -0.125 to 0.125
- down_weight: bfloat16 [2048, 16, 768], P('dp', 'expert'), may hold values from -0.21875 to 0.21875
Outputs:
- token_grad: bfloat16 [196608, 2048], P(('dp', 'expert'))
- gate_gradient: float32 [2048, 16, 768], P('dp', 'expert')
- up_gradient: float32 [2048, 16, 768], P('dp', 'expert')
- down_gradient: float32 [2048, 16, 768], P('dp', 'expert')
The draws below stay inside these ranges and needn't reach their ends.
Inputs may be any that keep to these rules, and one draw needn't show every extreme that they name: `route_index`: within each list of 16 slots the indices are distinct; each names a token of the source device. `route_count`: in every group one expert has all 16 slots live from every source device; slots at or beyond the count are unused.
All inputs are finite; a program needn't handle non-finite values.
Results may differ from the reference program's by a relative error of at most 0.0059.
Values may be sent and summed in bfloat16 or wider, within the bound.
No kernel may reach another device: no remote copies, remote signals or barrier semaphores. Data moves between devices by JAX's collectives and lax.ppermute only.
A program may use at most 128 MiB of HBM per device.

```python
import jax
import jax.numpy as jnp

D = 2048
FF = 768
TOK_DEV = 768
SLOTS = 16
GROUPS = 16
SOURCES = 16
EXPERTS = 16
TOKENS = 196608


def draw_route_count(key, part):
    keys_all = jax.random.split(jax.random.fold_in(key, 11), 3)
    shift_by = jax.random.randint(keys_all[0], (GROUPS, EXPERTS, 1), 0, 4).astype(jnp.int32)
    level_top = jnp.maximum(jnp.right_shift(jnp.full((GROUPS, EXPERTS, 1), SLOTS, jnp.int32), shift_by), 1)
    level_low = jnp.maximum(level_top // 2, 1)
    counts_drawn = jax.random.randint(keys_all[1], (GROUPS, EXPERTS, SOURCES), level_low, level_top + 1)
    full_expert = jax.random.randint(keys_all[2], (GROUPS, 1, 1), 0, EXPERTS)
    filled = jnp.where(jnp.arange(EXPERTS, dtype=jnp.int32)[None, :, None] == full_expert, SLOTS, counts_drawn)
    return filled.astype(jnp.int32)


def draw_route_index(key, part):
    keys_all = jax.random.split(jax.random.fold_in(key, 23), GROUPS * EXPERTS * SOURCES)
    chosen = jax.vmap(lambda subkey: jax.random.permutation(subkey, TOK_DEV)[:SLOTS])(keys_all)
    return chosen.reshape(GROUPS, EXPERTS, SOURCES, SLOTS).astype(jnp.int32)


def block_scale(own_key, dims, pieces, smallest, top_value):
    level = 1.0
    for position, parts in pieces:
        heights = jax.random.uniform(jax.random.fold_in(jax.random.fold_in(own_key, 6), position), (parts,), jnp.float32, smallest / len(pieces), top_value / len(pieces))
        level = level * jnp.repeat(jnp.exp(heights), dims[position] // parts).reshape((-1,) + (1,) * (len(dims) - 1 - position))
    return level


def scatter_about(own_key, shape, deviation, most, shards=(), held_as=jnp.bfloat16):
    gain = block_scale(own_key, shape, shards, -0.22, 0.18) if shards else 1.0
    array = jax.random.normal(own_key, shape, jnp.float32) * deviation * gain
    return jnp.minimum(jnp.maximum(array, -most), most).astype(held_as)


def setup_inputs(seed: int = 0) -> dict:
    splits = jax.random.split(jax.random.key(seed), 9)
    tokens = scatter_about(splits[0], (TOKENS, D), 1.0, 6.0, ((0, 256),))
    target = scatter_about(splits[1], (TOKENS, D), 0.5, 4.0, ((0, 256),))
    route_index = draw_route_index(jax.random.fold_in(splits[8], 71), 0)
    route_count = draw_route_count(jax.random.fold_in(splits[8], 71), 0)
    route_gate = jnp.clip(0.1 + 0.9 * jax.random.uniform(splits[4], (GROUPS, EXPERTS, SOURCES, SLOTS), jnp.float32) ** block_scale(splits[4], (GROUPS, EXPERTS, SOURCES, SLOTS), ((0, 16), (2, 16)), -0.2, 0.2), 0.1, 1.0)
    gate_weight = scatter_about(splits[5], (D, EXPERTS, FF), D ** -0.5, 0.125, ((0, 16), (1, 16)))
    up_weight = scatter_about(splits[6], (D, EXPERTS, FF), D ** -0.5, 0.125, ((0, 16), (1, 16)))
    down_weight = scatter_about(splits[7], (D, EXPERTS, FF), FF ** -0.5, 0.21875, ((0, 16), (1, 16)))
    return {"tokens": tokens, "target": target, "route_index": route_index, "route_count": route_count, "route_gate": route_gate, "gate_weight": gate_weight, "up_weight": up_weight, "down_weight": down_weight}


def reference(tokens, target, route_index, route_count, route_gate, gate_weight, up_weight, down_weight):
    groups, experts, sources, per_source = route_index.shape
    model_width = tokens.shape[1]
    device_tokens = tokens.shape[0] // (groups * sources)
    usable = jnp.arange(per_source, dtype=jnp.int32)[None, None, None, :] < route_count[:, :, :, None]
    offsets = (jnp.arange(groups, dtype=jnp.int32)[:, None, None, None] * sources + jnp.arange(sources, dtype=jnp.int32)[None, None, :, None]) * device_tokens
    slot_token = (offsets + route_index).astype(jnp.int32).reshape(groups, experts, sources * per_source)
    slot_weight = jnp.where(usable, route_gate, 0.0).astype(jnp.float32).reshape(groups, experts, sources * per_source)
    usable_rows = usable.reshape(groups, experts, sources * per_source)
    expert_rows = tokens[slot_token] * usable_rows[..., None].astype(tokens.dtype)
    rows_wide = expert_rows.astype(jnp.float32)
    gate_wide = gate_weight.astype(jnp.float32)
    up_wide = up_weight.astype(jnp.float32)
    down_wide = down_weight.astype(jnp.float32)
    gate_pre = jnp.einsum("gerd,def->gerf", rows_wide, gate_wide)
    up_pre = jnp.einsum("gerd,def->gerf", rows_wide, up_wide)
    sigma = jax.nn.sigmoid(gate_pre)
    active = gate_pre * sigma
    hidden = (active * up_pre).astype(jnp.bfloat16)
    expert_out = jnp.einsum("gerf,def->gerd", hidden.astype(jnp.float32), down_wide).astype(jnp.bfloat16)
    flat_token = slot_token.reshape(-1)
    combined = jnp.zeros((tokens.shape[0], model_width), jnp.float32).at[flat_token].add(
        (slot_weight[..., None] * expert_out.astype(jnp.float32)).reshape(-1, model_width))
    out_grad = combined - target.astype(jnp.float32)
    slot_grad = (slot_weight[..., None] * out_grad[slot_token]).astype(jnp.bfloat16)
    hidden_grad = jnp.einsum("gerd,def->gerf", slot_grad.astype(jnp.float32), down_wide)
    gate_grad = (hidden_grad * up_pre * sigma * (1.0 + gate_pre * (1.0 - sigma))).astype(jnp.bfloat16)
    up_grad = (hidden_grad * active).astype(jnp.bfloat16)
    row_grad = (jnp.einsum("gerf,def->gerd", gate_grad.astype(jnp.float32), gate_wide)
                + jnp.einsum("gerf,def->gerd", up_grad.astype(jnp.float32), up_wide)).astype(jnp.bfloat16)
    token_grad = jnp.zeros((tokens.shape[0], model_width), jnp.float32).at[flat_token].add(
        row_grad.astype(jnp.float32).reshape(-1, model_width)).astype(jnp.bfloat16)
    factor = (groups * sources * per_source) ** -0.5
    gate_gradient = jnp.einsum("gerd,gerf->def", rows_wide, gate_grad.astype(jnp.float32)) * factor
    up_gradient = jnp.einsum("gerd,gerf->def", rows_wide, up_grad.astype(jnp.float32)) * factor
    down_gradient = jnp.einsum("gerd,gerf->def", slot_grad.astype(jnp.float32), hidden.astype(jnp.float32)) * factor
    return token_grad, gate_gradient, up_gradient, down_gradient
```

```python
import jax
import jax.numpy as jnp
from jax import lax
from jax.sharding import PartitionSpec as P

F32 = jnp.float32
BF16 = jnp.bfloat16


def exchange(block):
    return lax.all_to_all(block, "expert", split_axis=0, concat_axis=0, tiled=True)


def dot(a, b, dims):
    return lax.dot_general(a, b, (dims, ((), ())), preferred_element_type=F32)


def on_device(
    tokens, target, route_index, route_count, route_gate, gate_weight, up_weight, down_weight
):
    groups = lax.axis_size("dp")
    sources = lax.axis_size("expert")
    local_index = route_index[0, :, 0, :]
    live_count = route_count[0, :, 0]
    per_source = local_index.shape[1]
    held, width = tokens.shape
    ff = gate_weight.shape[2]
    slots = sources * per_source

    with jax.named_scope("gather_weights"):
        own = jnp.concatenate([gate_weight[:, 0], up_weight[:, 0], down_weight[:, 0]], axis=1)
        full = lax.all_gather(own, "dp", axis=0, tiled=True)
        gate_up, down = full[:, : 2 * ff], full[:, 2 * ff :]

    with jax.named_scope("routing"):
        usable = jnp.arange(per_source, dtype=jnp.int32)[None, :] < live_count[:, None]
        flat_index = local_index.reshape(slots)
        live = usable.reshape(slots)
        weight = jnp.where(live, route_gate[0, :, 0, :].reshape(slots), 0.0)
        names = flat_index[:, None] == jnp.arange(held, dtype=jnp.int32)[None, :]
        pick = (names & live[:, None]).astype(BF16)
        same = flat_index[:, None] == flat_index[None, :]
        high = lax.reduce_precision(weight, 8, 7)
        low = weight - high
        mix_high = jnp.where(same, high[None, :], 0.0).astype(BF16)
        mix_low = jnp.where(same, low[None, :], 0.0).astype(BF16)

    with jax.named_scope("rows_out"):
        rows = dot(pick, tokens, ((1,), (0,))).astype(BF16)
        expert_rows = exchange(rows.reshape(sources, per_source, width)).reshape(slots, width)
        wanted = dot(pick, target, ((1,), (0,)))

    with jax.named_scope("forward"):
        pre = dot(expert_rows, gate_up, ((1,), (0,)))
        gate_pre, up_pre = pre[:, :ff], pre[:, ff:]
        sigma = jax.nn.sigmoid(gate_pre)
        active = gate_pre * sigma
        hidden = (active * up_pre).astype(BF16)
        expert_out = dot(hidden, down, ((1,), (1,))).astype(BF16)

    with jax.named_scope("combine"):
        returned = exchange(expert_out.reshape(sources, per_source, width)).reshape(slots, width)
        combined = dot(mix_high, returned, ((1,), (0,))) + dot(mix_low, returned, ((1,), (0,)))
        slot_grad = (weight[:, None] * (combined - wanted)).astype(BF16)
        owner_grad = exchange(slot_grad.reshape(sources, per_source, width)).reshape(slots, width)

    with jax.named_scope("backward"):
        hidden_grad = dot(owner_grad, down, ((1,), (0,)))
        gate_grad = (hidden_grad * up_pre * sigma * (1.0 + gate_pre * (1.0 - sigma))).astype(BF16)
        up_grad = (hidden_grad * active).astype(BF16)
        pre_grad = jnp.concatenate([gate_grad, up_grad], axis=1)

    with jax.named_scope("weight_gradients"):
        partial = jnp.concatenate(
            [
                dot(expert_rows, pre_grad, ((0,), (0,))).astype(BF16),
                dot(owner_grad, hidden, ((0,), (0,))).astype(BF16),
            ],
            axis=1,
        )
        summed = lax.psum_scatter(partial, "dp", scatter_dimension=0, tiled=True)
        scaled = summed.astype(F32) * (groups * sources * per_source) ** (-0.5)

    with jax.named_scope("token_gradient"):
        row_grad = dot(pre_grad, gate_up, ((1,), (1,))).astype(BF16)
        came_back = exchange(row_grad.reshape(sources, per_source, width)).reshape(slots, width)
        token_grad = dot(names.astype(BF16), came_back, ((0,), (0,))).astype(BF16)

    return (
        token_grad,
        scaled[:, None, :ff],
        scaled[:, None, ff : 2 * ff],
        scaled[:, None, 2 * ff :],
    )


def solution(mesh):
    return jax.shard_map(
        on_device,
        mesh=mesh,
        in_specs=(
            P(("dp", "expert"), None),
            P(("dp", "expert"), None),
            P("dp", None, "expert", None),
            P("dp", None, "expert"),
            P("dp", None, "expert", None),
            P("dp", "expert", None),
            P("dp", "expert", None),
            P("dp", "expert", None),
        ),
        out_specs=(
            P(("dp", "expert"), None),
            P("dp", "expert", None),
            P("dp", "expert", None),
            P("dp", "expert", None),
        ),
        check_vma=False,
    )
```

```python
import jax
import jax.numpy as jnp
from jax import lax
from jax.experimental import pallas as pl
from jax.experimental.pallas import tpu as pltpu
from jax.sharding import PartitionSpec as P

F32 = jnp.float32
BF16 = jnp.bfloat16
ROW_BY_ROW = ((1,), (0,))
OVER_LAST = ((1,), (1,))
OVER_FIRST = ((0,), (0,))
VMEM_LIMIT = 40 * 1024 * 1024


def exchange(block):
    return lax.all_to_all(block, "expert", split_axis=0, concat_axis=0, tiled=True)


def dot(a, b, dims):
    return lax.dot_general(a, b, (dims, ((), ())), preferred_element_type=F32)


def call(body, grid, in_specs, out_specs, out_shape, flops, moved, prefetch=0):
    return pl.pallas_call(
        body,
        grid_spec=pltpu.PrefetchScalarGridSpec(
            num_scalar_prefetch=prefetch, grid=grid, in_specs=in_specs, out_specs=out_specs
        ),
        out_shape=out_shape,
        compiler_params=pltpu.CompilerParams(vmem_limit_bytes=VMEM_LIMIT),
        cost_estimate=pl.CostEstimate(flops=flops, bytes_accessed=moved, transcendentals=0),
    )


def shape(rows, columns, dtype):
    return jax.ShapeDtypeStruct((rows, columns), dtype)


def project_in(rows, full, ff):
    slots, width = rows.shape
    wide = 256
    steps = ff // wide

    def body(x, wg, wu, gate_pre, up_pre, hidden):
        g = dot(x[...], wg[...], ROW_BY_ROW)
        u = dot(x[...], wu[...], ROW_BY_ROW)
        gate_pre[...] = g
        up_pre[...] = u
        hidden[...] = (g * jax.nn.sigmoid(g) * u).astype(BF16)

    part = pl.BlockSpec((slots, wide), lambda j: (0, j))
    return call(
        body,
        (steps,),
        [
            pl.BlockSpec((slots, width), lambda j: (0, 0)),
            pl.BlockSpec((width, wide), lambda j: (0, j)),
            pl.BlockSpec((width, wide), lambda j: (0, steps + j)),
        ],
        [part, part, part],
        [shape(slots, ff, F32), shape(slots, ff, F32), shape(slots, ff, BF16)],
        4 * slots * width * ff,
        4 * width * ff + 2 * slots * width + 10 * slots * ff,
    )(rows, full, full)


def project_out(hidden, full, ff):
    slots, width = hidden.shape[0], full.shape[0]
    tall = 512

    def body(h, wd, out):
        out[...] = dot(h[...], wd[...], OVER_LAST).astype(BF16)

    return call(
        body,
        (width // tall,),
        [
            pl.BlockSpec((slots, ff), lambda j: (0, 0)),
            pl.BlockSpec((tall, ff), lambda j: (j, 2)),
        ],
        pl.BlockSpec((slots, tall), lambda j: (0, j)),
        shape(slots, width, BF16),
        2 * slots * width * ff,
        2 * width * ff + 2 * slots * (width + ff),
    )(hidden, full)


def back_in(owner_grad, full, gate_pre, up_pre, ff):
    slots, width = owner_grad.shape
    wide = 256
    steps = ff // wide

    def body(x, wd, gate_ref, up_ref, gate_grad, up_grad):
        h = dot(x[...], wd[...], ROW_BY_ROW)
        g = gate_ref[...]
        sig = jax.nn.sigmoid(g)
        gate_grad[...] = (h * up_ref[...] * sig * (1.0 + g * (1.0 - sig))).astype(BF16)
        up_grad[...] = (h * (g * sig)).astype(BF16)

    part = pl.BlockSpec((slots, wide), lambda j: (0, j))
    return call(
        body,
        (steps,),
        [
            pl.BlockSpec((slots, width), lambda j: (0, 0)),
            pl.BlockSpec((width, wide), lambda j: (0, 2 * steps + j)),
            part,
            part,
        ],
        [part, part],
        [shape(slots, ff, BF16), shape(slots, ff, BF16)],
        2 * slots * width * ff,
        2 * width * ff + 2 * slots * width + 12 * slots * ff,
    )(owner_grad, full, gate_pre, up_pre)


def back_out(gate_grad, up_grad, full, ff):
    slots, width = gate_grad.shape[0], full.shape[0]
    tall = 512

    def body(g, u, wg, wu, out):
        out[...] = (
            dot(g[...], wg[...], OVER_LAST) + dot(u[...], wu[...], OVER_LAST)
        ).astype(BF16)

    return call(
        body,
        (width // tall,),
        [
            pl.BlockSpec((slots, ff), lambda j: (0, 0)),
            pl.BlockSpec((slots, ff), lambda j: (0, 0)),
            pl.BlockSpec((tall, ff), lambda j: (j, 0)),
            pl.BlockSpec((tall, ff), lambda j: (j, 1)),
        ],
        pl.BlockSpec((slots, tall), lambda j: (0, j)),
        shape(slots, width, BF16),
        4 * slots * width * ff,
        4 * width * ff + 2 * slots * (width + 2 * ff),
    )(gate_grad, up_grad, full, full)


def chip_gradient(blocks, own, other, dtype):
    count = blocks.shape[0]
    slots, ff = own[1].shape
    tall = 128

    def body(names, xa, ga, ua, oa, ha, xb, gb, ub, ob, hb, out):
        xa, xb, oa, ob = xa[...], xb[...], oa[...], ob[...]
        gate = dot(xa, ga[...], OVER_FIRST) + dot(xb, gb[...], OVER_FIRST)
        up = dot(xa, ua[...], OVER_FIRST) + dot(xb, ub[...], OVER_FIRST)
        down = dot(oa, ha[...], OVER_FIRST) + dot(ob, hb[...], OVER_FIRST)
        out[0, :, :ff] = gate.astype(dtype)
        out[0, :, ff : 2 * ff] = up.astype(dtype)
        out[0, :, 2 * ff :] = down.astype(dtype)

    column = pl.BlockSpec((slots, tall), lambda i, names: (0, names[i]))
    whole = pl.BlockSpec((slots, ff), lambda i, names: (0, 0))
    return call(
        body,
        (count,),
        [column, whole, whole, column, whole] * 2,
        pl.BlockSpec((1, tall, 3 * ff), lambda i, names: (i, 0, 0)),
        jax.ShapeDtypeStruct((count, tall, 3 * ff), dtype),
        12 * count * slots * tall * ff,
        12 * slots * ff + count * (8 * slots * tall + 12 * tall * ff),
        prefetch=1,
    )(blocks, *own, *other)


def last_sum(first, second, mine, ff, factor):
    tall = mine.shape[0]

    def body(a, b, c, gate, up, down):
        s = (a[...].astype(F32) + b[...].astype(F32) + c[...]) * factor
        gate[...] = s[:, :ff]
        up[...] = s[:, ff : 2 * ff]
        down[...] = s[:, 2 * ff :]

    block = pl.BlockSpec((tall, 3 * ff), lambda i: (0, 0))
    part = pl.BlockSpec((tall, ff), lambda i: (0, 0))
    return call(
        body, (1,), [block] * 3, [part] * 3, [shape(tall, ff, F32)] * 3, 12 * tall * ff, 36 * tall * ff
    )(first, second, mine)


def on_device(
    tokens, target, route_index, route_count, route_gate, gate_weight, up_weight, down_weight
):
    groups = lax.axis_size("dp")
    sources = lax.axis_size("expert")
    chips = groups // 2
    local_index = route_index[0, :, 0, :]
    live_count = route_count[0, :, 0]
    per_source = local_index.shape[1]
    held, width = tokens.shape
    tall = gate_weight.shape[0]
    ff = gate_weight.shape[2]
    slots = sources * per_source

    def along(array, by):
        pairs = [
            (2 * z + c, 2 * ((z + by) % chips) + c) for z in range(chips) for c in range(2)
        ]
        return lax.ppermute(array, "dp", pairs)

    def other_core(array):
        return lax.ppermute(array, "dp", [(d, d ^ 1) for d in range(groups)])

    with jax.named_scope("gather_weights"):
        own = jnp.concatenate([gate_weight[:, 0], up_weight[:, 0], down_weight[:, 0]], axis=1)
        full = lax.all_gather(own, "dp", axis=0, tiled=True)

    with jax.named_scope("routing"):
        usable = jnp.arange(per_source, dtype=jnp.int32)[None, :] < live_count[:, None]
        flat_index = local_index.reshape(slots)
        live = usable.reshape(slots)
        weight = jnp.where(live, route_gate[0, :, 0, :].reshape(slots), 0.0)
        names = flat_index[:, None] == jnp.arange(held, dtype=jnp.int32)[None, :]
        pick = (names & live[:, None]).astype(BF16)
        same = flat_index[:, None] == flat_index[None, :]
        high = lax.reduce_precision(weight, 8, 7)
        low = weight - high
        mix_high = jnp.where(same, high[None, :], 0.0).astype(BF16)
        mix_low = jnp.where(same, low[None, :], 0.0).astype(BF16)

    with jax.named_scope("rows_out"):
        rows = dot(pick, tokens, ROW_BY_ROW).astype(BF16)
        expert_rows = exchange(rows.reshape(sources, per_source, width)).reshape(slots, width)
        other_rows = other_core(expert_rows)
        wanted = dot(pick, target, ROW_BY_ROW)

    with jax.named_scope("forward"):
        gate_pre, up_pre, hidden = project_in(expert_rows, full, ff)
        expert_out = project_out(hidden, full, ff)
        other_hidden = other_core(hidden)

    with jax.named_scope("combine"):
        returned = exchange(expert_out.reshape(sources, per_source, width)).reshape(slots, width)
        combined = dot(mix_high, returned, ROW_BY_ROW) + dot(mix_low, returned, ROW_BY_ROW)
        slot_grad = (weight[:, None] * (combined - wanted)).astype(BF16)
        owner_grad = exchange(slot_grad.reshape(sources, per_source, width)).reshape(slots, width)
        other_grad = other_core(owner_grad)

    with jax.named_scope("backward"):
        gate_grad, up_grad = back_in(owner_grad, full, gate_pre, up_pre, ff)
        other_gate, other_up = other_core(gate_grad), other_core(up_grad)

    with jax.named_scope("weight_gradients"):
        place = lax.axis_index("dp")
        z, core = place // 2, place % 2
        mine = (expert_rows, gate_grad, up_grad, owner_grad, hidden)
        theirs = (other_rows, other_gate, other_up, other_grad, other_hidden)

        def terms(steps, dtype=F32):
            blocks = jnp.stack([((z + s) % chips) * 2 + core for s in steps]).astype(jnp.int32)
            return chip_gradient(blocks, mine, theirs, dtype)

        half = tall // 2
        far = chips // 2
        farthest = terms([far], BF16)[0]
        ahead, behind = along(farthest[:half], 1), along(farthest[half:], -1)
        for step in range(far - 1, 0, -1):
            both = terms([step, chips - step])
            if step == far - 1:
                first = jnp.concatenate([both[0, :half] + ahead.astype(F32), both[0, half:]], axis=0)
                second = jnp.concatenate([both[1, :half], both[1, half:] + behind.astype(F32)], axis=0)
            else:
                first, second = both[0] + ahead.astype(F32), both[1] + behind.astype(F32)
            ahead, behind = along(first.astype(BF16), 1), along(second.astype(BF16), -1)
        factor = (groups * sources * per_source) ** (-0.5)
        gradients = last_sum(ahead, behind, terms([0])[0], ff, factor)

    with jax.named_scope("token_gradient"):
        row_grad = back_out(gate_grad, up_grad, full, ff)
        came_back = exchange(row_grad.reshape(sources, per_source, width)).reshape(slots, width)
        token_grad = dot(names.astype(BF16), came_back, OVER_FIRST).astype(BF16)

    return (token_grad, *(g[:, None, :] for g in gradients))


def solution(mesh):
    return jax.shard_map(
        on_device,
        mesh=mesh,
        in_specs=(
            P(("dp", "expert"), None),
            P(("dp", "expert"), None),
            P("dp", None, "expert", None),
            P("dp", None, "expert"),
            P("dp", None, "expert", None),
            P("dp", "expert", None),
            P("dp", "expert", None),
            P("dp", "expert", None),
        ),
        out_specs=(
            P(("dp", "expert"), None),
            P("dp", "expert", None),
            P("dp", "expert", None),
            P("dp", "expert", None),
        ),
        check_vma=False,
    )
```

```python
import jax
import jax.numpy as jnp
from jax import lax
from jax.experimental import pallas as pl
from jax.experimental.pallas import tpu as pltpu
from jax.sharding import PartitionSpec as P

F32 = jnp.float32
BF16 = jnp.bfloat16
ROW_BY_ROW = ((1,), (0,))
OVER_LAST = ((1,), (1,))
OVER_FIRST = ((0,), (0,))
MIB = 1024 * 1024
VMEM_LIMIT = 24 * MIB


def exchange(block):
    return lax.all_to_all(block, "expert", split_axis=0, concat_axis=0, tiled=True)


def dot(a, b, dims):
    return lax.dot_general(a, b, (dims, ((), ())), preferred_element_type=F32)


def in_hbm(array):
    return pltpu.with_memory_space_constraint(array, pltpu.HBM)


def call(body, grid, in_specs, out_specs, out_shape, flops, moved, prefetch=0, limit=VMEM_LIMIT):
    return pl.pallas_call(
        body,
        grid_spec=pltpu.PrefetchScalarGridSpec(
            num_scalar_prefetch=prefetch, grid=grid, in_specs=in_specs, out_specs=out_specs
        ),
        out_shape=out_shape,
        compiler_params=pltpu.CompilerParams(vmem_limit_bytes=limit),
        cost_estimate=pl.CostEstimate(flops=flops, bytes_accessed=moved, transcendentals=0),
    )


def side_by_side(gate_weight, up_weight, down_weight):
    tall, ff = gate_weight.shape

    def body(g, u, d, out):
        out[:, :ff] = g[...]
        out[:, ff : 2 * ff] = u[...]
        out[:, 2 * ff :] = d[...]

    part = pl.BlockSpec((tall, ff), lambda i: (0, 0))
    return call(
        body,
        (1,),
        [part] * 3,
        pl.BlockSpec((tall, 3 * ff), lambda i: (0, 0)),
        shape(tall, 3 * ff, BF16),
        0,
        12 * tall * ff,
    )(gate_weight, up_weight, down_weight)


def shape(rows, columns, dtype):
    return jax.ShapeDtypeStruct((rows, columns), dtype)


def project_in(rows, full, ff):
    slots, width = rows.shape
    wide = 256
    steps = ff // wide

    def body(x, wg, wu, gate_pre, up_pre, hidden):
        g = dot(x[...], wg[...], ROW_BY_ROW)
        u = dot(x[...], wu[...], ROW_BY_ROW)
        gate_pre[...] = g
        up_pre[...] = u
        hidden[...] = (g * jax.nn.sigmoid(g) * u).astype(BF16)

    part = pl.BlockSpec((slots, wide), lambda j: (0, j))
    return call(
        body,
        (steps,),
        [
            pl.BlockSpec((slots, width), lambda j: (0, 0)),
            pl.BlockSpec((width, wide), lambda j: (0, j)),
            pl.BlockSpec((width, wide), lambda j: (0, steps + j)),
        ],
        [part, part, part],
        [shape(slots, ff, F32), shape(slots, ff, F32), shape(slots, ff, BF16)],
        4 * slots * width * ff,
        4 * width * ff + 2 * slots * width + 10 * slots * ff,
    )(rows, in_hbm(full), in_hbm(full))


def project_out(hidden, full, ff):
    slots, width = hidden.shape[0], full.shape[0]
    tall = 512

    def body(h, wd, out):
        out[...] = dot(h[...], wd[...], OVER_LAST).astype(BF16)

    return call(
        body,
        (width // tall,),
        [
            pl.BlockSpec((slots, ff), lambda j: (0, 0)),
            pl.BlockSpec((tall, ff), lambda j: (j, 2)),
        ],
        pl.BlockSpec((slots, tall), lambda j: (0, j)),
        shape(slots, width, BF16),
        2 * slots * width * ff,
        2 * width * ff + 2 * slots * (width + ff),
    )(hidden, in_hbm(full))


def combine(mix_high, mix_low, weight, returned, wanted):
    slots, width = returned.shape
    wide = 512

    def body(high, low, w, back, goal, out):
        x = back[...]
        total = dot(high[...], x, ROW_BY_ROW) + dot(low[...], x, ROW_BY_ROW)
        out[...] = (w[...] * (total - goal[...].astype(F32))).astype(BF16)

    mix = pl.BlockSpec((slots, slots), lambda j: (0, 0))
    part = pl.BlockSpec((slots, wide), lambda j: (0, j))
    return call(
        body,
        (width // wide,),
        [mix, mix, pl.BlockSpec((slots, 1), lambda j: (0, 0)), part, part],
        part,
        shape(slots, width, BF16),
        4 * slots * slots * width,
        6 * slots * width,
    )(mix_high, mix_low, weight, returned, wanted)


def back_in(owner_grad, full, gate_pre, up_pre, ff):
    slots, width = owner_grad.shape
    wide = 256
    steps = ff // wide

    def body(x, wd, gate_ref, up_ref, out):
        h = dot(x[...], wd[...], ROW_BY_ROW)
        g = gate_ref[...]
        sig = jax.nn.sigmoid(g)
        out[0] = (h * up_ref[...] * sig * (1.0 + g * (1.0 - sig))).astype(BF16)
        out[1] = (h * (g * sig)).astype(BF16)

    part = pl.BlockSpec((slots, wide), lambda j: (0, j))
    return call(
        body,
        (steps,),
        [
            pl.BlockSpec((slots, width), lambda j: (0, 0)),
            pl.BlockSpec((width, wide), lambda j: (0, 2 * steps + j)),
            part,
            part,
        ],
        pl.BlockSpec((2, slots, wide), lambda j: (0, 0, j)),
        jax.ShapeDtypeStruct((2, slots, ff), BF16),
        2 * slots * width * ff,
        2 * width * ff + 2 * slots * width + 12 * slots * ff,
    )(owner_grad, in_hbm(full), gate_pre, up_pre)


def back_out(pre_grad, full, ff):
    slots, width = pre_grad.shape[1], full.shape[0]
    tall = 512

    def body(x, wg, wu, out):
        out[...] = (
            dot(x[0], wg[...], OVER_LAST) + dot(x[1], wu[...], OVER_LAST)
        ).astype(BF16)

    return call(
        body,
        (width // tall,),
        [
            pl.BlockSpec((2, slots, ff), lambda j: (0, 0, 0)),
            pl.BlockSpec((tall, ff), lambda j: (j, 0)),
            pl.BlockSpec((tall, ff), lambda j: (j, 1)),
        ],
        pl.BlockSpec((slots, tall), lambda j: (0, j)),
        shape(slots, width, BF16),
        4 * slots * width * ff,
        4 * width * ff + 2 * slots * (width + 2 * ff),
    )(pre_grad, in_hbm(full), in_hbm(full))


def chip_terms(blocks, own, other, halves):
    count = blocks.shape[0]
    slots, ff = own[3].shape
    tall = 128

    def body(names, xa, pa, oa, ha, xb, pb, ob, hb, *outs):
        xa, xb, oa, ob = xa[...], xb[...], oa[...], ob[...]
        gate = dot(xa, pa[0], OVER_FIRST) + dot(xb, pb[0], OVER_FIRST)
        up = dot(xa, pa[1], OVER_FIRST) + dot(xb, pb[1], OVER_FIRST)
        down = dot(oa, ha[...], OVER_FIRST) + dot(ob, hb[...], OVER_FIRST)
        for at, part in ((0, gate), (ff, up), (2 * ff, down)):
            if halves:
                outs[0][:, at : at + ff] = part[: tall // 2].astype(BF16)
                outs[1][:, at : at + ff] = part[tall // 2 :].astype(BF16)
            else:
                outs[0][0, :, at : at + ff] = part

    column = pl.BlockSpec((slots, tall), lambda i, names: (0, names[i]))
    pair = pl.BlockSpec((2, slots, ff), lambda i, names: (0, 0, 0))
    whole = pl.BlockSpec((slots, ff), lambda i, names: (0, 0))
    if halves:
        out_specs = [pl.BlockSpec((tall // 2, 3 * ff), lambda i, names: (0, 0))] * 2
        out_shape = [shape(tall // 2, 3 * ff, BF16)] * 2
    else:
        out_specs = pl.BlockSpec((1, tall, 3 * ff), lambda i, names: (i, 0, 0))
        out_shape = jax.ShapeDtypeStruct((count, tall, 3 * ff), F32)
    return call(
        body,
        (count,),
        [column, pair, column, whole] * 2,
        out_specs,
        out_shape,
        12 * count * slots * tall * ff,
        12 * slots * ff + count * (8 * slots * tall + 12 * tall * ff),
        prefetch=1,
    )(blocks, *own, *other)


def add_terms(ahead, behind, terms, at):
    tall, width = terms.shape[1:]
    part = ahead.shape[0]

    def body(a, b, first, second, out_a, out_b):
        if part == tall:
            out_a[...] = (first[0] + a[...].astype(F32)).astype(BF16)
            out_b[...] = (second[0] + b[...].astype(F32)).astype(BF16)
        else:
            out_a[:part] = (first[0, :part] + a[...].astype(F32)).astype(BF16)
            out_a[part:] = first[0, part:].astype(BF16)
            out_b[:part] = second[0, :part].astype(BF16)
            out_b[part:] = (second[0, part:] + b[...].astype(F32)).astype(BF16)

    came = pl.BlockSpec((part, width), lambda i: (0, 0))
    sent = pl.BlockSpec((tall, width), lambda i: (0, 0))
    return call(
        body,
        (1,),
        [
            came,
            came,
            pl.BlockSpec((1, tall, width), lambda i: (at, 0, 0)),
            pl.BlockSpec((1, tall, width), lambda i: (at + 1, 0, 0)),
        ],
        [sent, sent],
        [shape(tall, width, BF16)] * 2,
        2 * tall * width,
        16 * tall * width,
    )(ahead, behind, terms, terms)


def last_sum(ahead, behind, terms, at, ff, factor):
    tall = ahead.shape[0]

    def body(a, b, mine, gate, up, down):
        total = (a[...].astype(F32) + b[...].astype(F32) + mine[0]) * factor
        gate[:, 0, :] = total[:, :ff]
        up[:, 0, :] = total[:, ff : 2 * ff]
        down[:, 0, :] = total[:, 2 * ff :]

    came = pl.BlockSpec((tall, 3 * ff), lambda i: (0, 0))
    part = pl.BlockSpec((tall, 1, ff), lambda i: (0, 0, 0))
    return call(
        body,
        (1,),
        [came, came, pl.BlockSpec((1, tall, 3 * ff), lambda i: (at, 0, 0))],
        [part] * 3,
        [jax.ShapeDtypeStruct((tall, 1, ff), F32)] * 3,
        12 * tall * ff,
        36 * tall * ff,
    )(ahead, behind, terms)


def to_tokens(names, came_back):
    held, slots = names.shape
    width = came_back.shape[1]
    wide = 512

    def body(which, back, out):
        out[...] = dot(which[...], back[...], ROW_BY_ROW).astype(BF16)

    return call(
        body,
        (width // wide,),
        [
            pl.BlockSpec((held, slots), lambda j: (0, 0)),
            pl.BlockSpec((slots, wide), lambda j: (0, j)),
        ],
        pl.BlockSpec((held, wide), lambda j: (0, j)),
        shape(held, width, BF16),
        2 * held * slots * width,
        2 * (held + slots) * width,
    )(names, came_back)


def on_device(
    tokens, target, route_index, route_count, route_gate, gate_weight, up_weight, down_weight
):
    groups = lax.axis_size("dp")
    sources = lax.axis_size("expert")
    chips = groups // 2
    local_index = route_index[0, :, 0, :]
    live_count = route_count[0, :, 0]
    per_source = local_index.shape[1]
    held, width = tokens.shape
    tall = gate_weight.shape[0]
    ff = gate_weight.shape[2]
    slots = sources * per_source

    def along(array, by):
        pairs = [
            (2 * z + c, 2 * ((z + by) % chips) + c) for z in range(chips) for c in range(2)
        ]
        return lax.ppermute(array, "dp", pairs)

    def other_core(array):
        return lax.ppermute(array, "dp", [(d, d ^ 1) for d in range(groups)])

    with jax.named_scope("gather_weights"):
        own = side_by_side(gate_weight[:, 0], up_weight[:, 0], down_weight[:, 0])
        full = lax.all_gather(own, "dp", axis=0, tiled=True)

    with jax.named_scope("routing"):
        usable = jnp.arange(per_source, dtype=jnp.int32)[None, :] < live_count[:, None]
        flat_index = local_index.reshape(slots)
        live = usable.reshape(slots)
        weight = jnp.where(live, route_gate[0, :, 0, :].reshape(slots), 0.0)
        names = flat_index[:, None] == jnp.arange(held, dtype=jnp.int32)[None, :]
        pick = (names & live[:, None]).astype(BF16)
        same = flat_index[:, None] == flat_index[None, :]
        high = lax.reduce_precision(weight, 8, 7)
        low = weight - high
        mix_high = jnp.where(same, high[None, :], 0.0).astype(BF16)
        mix_low = jnp.where(same, low[None, :], 0.0).astype(BF16)

    with jax.named_scope("rows_out"):
        rows = dot(pick, tokens, ROW_BY_ROW).astype(BF16)
        expert_rows = exchange(rows.reshape(sources, per_source, width)).reshape(slots, width)
        other_rows = other_core(expert_rows)
        wanted = dot(pick, target, ROW_BY_ROW).astype(BF16)

    with jax.named_scope("forward"):
        gate_pre, up_pre, hidden = project_in(expert_rows, full, ff)
        expert_out = project_out(hidden, full, ff)
        other_hidden = other_core(hidden)

    with jax.named_scope("combine"):
        returned = exchange(expert_out.reshape(sources, per_source, width)).reshape(slots, width)
        slot_grad = combine(mix_high, mix_low, weight[:, None], returned, wanted)
        owner_grad = exchange(slot_grad.reshape(sources, per_source, width)).reshape(slots, width)
        other_grad = other_core(owner_grad)

    with jax.named_scope("backward"):
        pre_grad = back_in(owner_grad, full, gate_pre, up_pre, ff)
        other_pre = other_core(pre_grad)

    with jax.named_scope("weight_gradients"):
        place = lax.axis_index("dp")
        z, core = place // 2, place % 2
        mine = (expert_rows, pre_grad, owner_grad, hidden)
        theirs = (other_rows, other_pre, other_grad, other_hidden)
        far = chips // 2
        steps = [s for near in range(far - 1, 0, -1) for s in (near, chips - near)] + [0]
        blocks = ((z + jnp.array([far] + steps, jnp.int32)) & (chips - 1)) * 2 + core
        ahead, behind = chip_terms(blocks[:1], mine, theirs, True)
        ahead, behind = along(ahead, 1), along(behind, -1)
        terms = chip_terms(blocks[1:], mine, theirs, False)
        for at in range(0, len(steps) - 1, 2):
            ahead, behind = add_terms(ahead, behind, terms, at)
            ahead, behind = along(ahead, 1), along(behind, -1)
        factor = (groups * sources * per_source) ** (-0.5)
        gradients = last_sum(ahead, behind, terms, len(steps) - 1, ff, factor)

    with jax.named_scope("token_gradient"):
        row_grad = back_out(pre_grad, full, ff)
        came_back = exchange(row_grad.reshape(sources, per_source, width)).reshape(slots, width)
        token_grad = to_tokens(names.T.astype(BF16), came_back)

    return (token_grad, *gradients)


def solution(mesh):
    return jax.shard_map(
        on_device,
        mesh=mesh,
        in_specs=(
            P(("dp", "expert"), None),
            P(("dp", "expert"), None),
            P("dp", None, "expert", None),
            P("dp", None, "expert"),
            P("dp", None, "expert", None),
            P("dp", "expert", None),
            P("dp", "expert", None),
            P("dp", "expert", None),
        ),
        out_specs=(
            P(("dp", "expert"), None),
            P("dp", "expert", None),
            P("dp", "expert", None),
            P("dp", "expert", None),
        ),
        check_vma=False,
    )
```

```python
import jax
import jax.numpy as jnp
from jax import lax
from jax.experimental import pallas as pl
from jax.experimental.pallas import tpu as pltpu
from jax.sharding import PartitionSpec as P

F32 = jnp.float32
BF16 = jnp.bfloat16
ROW_BY_ROW = ((1,), (0,))
OVER_LAST = ((1,), (1,))
OVER_FIRST = ((0,), (0,))
MIB = 1024 * 1024
VMEM_LIMIT = 24 * MIB


def exchange(block):
    return lax.all_to_all(block, "expert", split_axis=0, concat_axis=0, tiled=True)


def dot(a, b, dims):
    return lax.dot_general(a, b, (dims, ((), ())), preferred_element_type=F32)


def in_hbm(array):
    return pltpu.with_memory_space_constraint(array, pltpu.HBM)


def held_in_hbm(dims, dtype):
    return pltpu.HBM(dims, dtype)


def call(body, grid, in_specs, out_specs, out_shape, flops, moved, prefetch=0, limit=VMEM_LIMIT):
    return pl.pallas_call(
        body,
        grid_spec=pltpu.PrefetchScalarGridSpec(
            num_scalar_prefetch=prefetch, grid=grid, in_specs=in_specs, out_specs=out_specs
        ),
        out_shape=out_shape,
        compiler_params=pltpu.CompilerParams(vmem_limit_bytes=limit),
        cost_estimate=pl.CostEstimate(flops=flops, bytes_accessed=moved, transcendentals=0),
    )


def side_by_side(gate_weight, up_weight, down_weight):
    tall, ff = gate_weight.shape

    def body(g, u, d, out):
        out[:, :ff] = g[...]
        out[:, ff : 2 * ff] = u[...]
        out[:, 2 * ff :] = d[...]

    part = pl.BlockSpec((tall, ff), lambda i: (0, 0))
    return call(
        body,
        (1,),
        [part] * 3,
        pl.BlockSpec((tall, 3 * ff), lambda i: (0, 0)),
        held_in_hbm((tall, 3 * ff), BF16),
        0,
        12 * tall * ff,
    )(in_hbm(gate_weight), in_hbm(up_weight), in_hbm(down_weight))


def shape(rows, columns, dtype):
    return jax.ShapeDtypeStruct((rows, columns), dtype)


def project_in(rows, full, ff):
    slots, width = rows.shape
    wide = 256
    steps = ff // wide

    def body(x, wg, wu, gate_pre, up_pre, hidden):
        g = dot(x[...], wg[...], ROW_BY_ROW)
        u = dot(x[...], wu[...], ROW_BY_ROW)
        gate_pre[...] = g
        up_pre[...] = u
        hidden[...] = (g * jax.nn.sigmoid(g) * u).astype(BF16)

    part = pl.BlockSpec((slots, wide), lambda j: (0, j))
    return call(
        body,
        (steps,),
        [
            pl.BlockSpec((slots, width), lambda j: (0, 0)),
            pl.BlockSpec((width, wide), lambda j: (0, j)),
            pl.BlockSpec((width, wide), lambda j: (0, steps + j)),
        ],
        [part, part, part],
        [held_in_hbm((slots, ff), F32), held_in_hbm((slots, ff), F32), shape(slots, ff, BF16)],
        4 * slots * width * ff,
        4 * width * ff + 2 * slots * width + 10 * slots * ff,
    )(rows, in_hbm(full), in_hbm(full))


def project_out(hidden, full, ff):
    slots, width = hidden.shape[0], full.shape[0]
    tall = 512

    def body(h, wd, out):
        out[...] = dot(h[...], wd[...], OVER_LAST).astype(BF16)

    return call(
        body,
        (width // tall,),
        [
            pl.BlockSpec((slots, ff), lambda j: (0, 0)),
            pl.BlockSpec((tall, ff), lambda j: (j, 2)),
        ],
        pl.BlockSpec((slots, tall), lambda j: (0, j)),
        held_in_hbm((slots, width), BF16),
        2 * slots * width * ff,
        2 * width * ff + 2 * slots * (width + ff),
    )(hidden, in_hbm(full))


def combine(mix_high, mix_low, weight, returned, wanted):
    slots, width = returned.shape
    wide = 512

    def body(high, low, w, back, goal, out):
        x = back[...]
        total = dot(high[...], x, ROW_BY_ROW) + dot(low[...], x, ROW_BY_ROW)
        out[...] = (w[...] * (total - goal[...].astype(F32))).astype(BF16)

    mix = pl.BlockSpec((slots, slots), lambda j: (0, 0))
    part = pl.BlockSpec((slots, wide), lambda j: (0, j))
    return call(
        body,
        (width // wide,),
        [mix, mix, pl.BlockSpec((slots, 1), lambda j: (0, 0)), part, part],
        part,
        held_in_hbm((slots, width), BF16),
        4 * slots * slots * width,
        6 * slots * width,
    )(in_hbm(mix_high), in_hbm(mix_low), in_hbm(weight), in_hbm(returned), in_hbm(wanted))


def back_in(owner_grad, full, gate_pre, up_pre, ff):
    slots, width = owner_grad.shape
    wide = 256
    steps = ff // wide

    def body(x, wd, gate_ref, up_ref, out):
        h = dot(x[...], wd[...], ROW_BY_ROW)
        g = gate_ref[...]
        sig = jax.nn.sigmoid(g)
        out[0] = (h * up_ref[...] * sig * (1.0 + g * (1.0 - sig))).astype(BF16)
        out[1] = (h * (g * sig)).astype(BF16)

    part = pl.BlockSpec((slots, wide), lambda j: (0, j))
    return call(
        body,
        (steps,),
        [
            pl.BlockSpec((slots, width), lambda j: (0, 0)),
            pl.BlockSpec((width, wide), lambda j: (0, 2 * steps + j)),
            part,
            part,
        ],
        pl.BlockSpec((2, slots, wide), lambda j: (0, 0, j)),
        jax.ShapeDtypeStruct((2, slots, ff), BF16),
        2 * slots * width * ff,
        2 * width * ff + 2 * slots * width + 12 * slots * ff,
    )(in_hbm(owner_grad), in_hbm(full), in_hbm(gate_pre), in_hbm(up_pre))


def back_out(pre_grad, full, ff):
    slots, width = pre_grad.shape[1], full.shape[0]
    tall = 512

    def body(x, wg, wu, out):
        out[...] = (
            dot(x[0], wg[...], OVER_LAST) + dot(x[1], wu[...], OVER_LAST)
        ).astype(BF16)

    return call(
        body,
        (width // tall,),
        [
            pl.BlockSpec((2, slots, ff), lambda j: (0, 0, 0)),
            pl.BlockSpec((tall, ff), lambda j: (j, 0)),
            pl.BlockSpec((tall, ff), lambda j: (j, 1)),
        ],
        pl.BlockSpec((slots, tall), lambda j: (0, j)),
        held_in_hbm((slots, width), BF16),
        4 * slots * width * ff,
        4 * width * ff + 2 * slots * (width + 2 * ff),
    )(pre_grad, in_hbm(full), in_hbm(full))


def chip_terms(blocks, own, other, halves):
    count = blocks.shape[0]
    slots, ff = own[3].shape
    tall = 128

    def body(names, xa, pa, oa, ha, xb, pb, ob, hb, *outs):
        xa, xb, oa, ob = xa[...], xb[...], oa[...], ob[...]
        gate = dot(xa, pa[0], OVER_FIRST) + dot(xb, pb[0], OVER_FIRST)
        up = dot(xa, pa[1], OVER_FIRST) + dot(xb, pb[1], OVER_FIRST)
        down = dot(oa, ha[...], OVER_FIRST) + dot(ob, hb[...], OVER_FIRST)
        for at, part in ((0, gate), (ff, up), (2 * ff, down)):
            if halves:
                outs[0][:, at : at + ff] = part[: tall // 2].astype(BF16)
                outs[1][:, at : at + ff] = part[tall // 2 :].astype(BF16)
            else:
                outs[0][0, :, at : at + ff] = part

    column = pl.BlockSpec((slots, tall), lambda i, names: (0, names[i]))
    pair = pl.BlockSpec((2, slots, ff), lambda i, names: (0, 0, 0))
    whole = pl.BlockSpec((slots, ff), lambda i, names: (0, 0))
    if halves:
        out_specs = [pl.BlockSpec((tall // 2, 3 * ff), lambda i, names: (0, 0))] * 2
        out_shape = [shape(tall // 2, 3 * ff, BF16)] * 2
    else:
        out_specs = pl.BlockSpec((1, tall, 3 * ff), lambda i, names: (i, 0, 0))
        out_shape = held_in_hbm((count, tall, 3 * ff), F32)
    return call(
        body,
        (count,),
        [column, pair, column, whole] * 2,
        out_specs,
        out_shape,
        12 * count * slots * tall * ff,
        12 * slots * ff + count * (8 * slots * tall + 12 * tall * ff),
        prefetch=1,
    )(blocks, *own, *other)


def add_terms(ahead, behind, terms, at):
    tall, width = terms.shape[1:]
    part = ahead.shape[0]

    def body(a, b, first, second, out_a, out_b):
        if part == tall:
            out_a[...] = (first[0] + a[...].astype(F32)).astype(BF16)
            out_b[...] = (second[0] + b[...].astype(F32)).astype(BF16)
        else:
            out_a[:part] = (first[0, :part] + a[...].astype(F32)).astype(BF16)
            out_a[part:] = first[0, part:].astype(BF16)
            out_b[:part] = second[0, :part].astype(BF16)
            out_b[part:] = (second[0, part:] + b[...].astype(F32)).astype(BF16)

    wide = width // 3
    came = pl.BlockSpec((part, wide), lambda i: (0, i))
    sent = pl.BlockSpec((tall, wide), lambda i: (0, i))
    return call(
        body,
        (3,),
        [
            came,
            came,
            pl.BlockSpec((1, tall, wide), lambda i: (at, 0, i)),
            pl.BlockSpec((1, tall, wide), lambda i: (at + 1, 0, i)),
        ],
        [sent, sent],
        [shape(tall, width, BF16)] * 2,
        2 * tall * width,
        16 * tall * width,
    )(ahead, behind, in_hbm(terms), in_hbm(terms))


def last_sum(ahead, behind, terms, at, ff, factor):
    tall = ahead.shape[0]

    def body(a, b, mine, gate, up, down):
        total = (a[...].astype(F32) + b[...].astype(F32) + mine[0]) * factor
        gate[:, 0, :] = total[:, :ff]
        up[:, 0, :] = total[:, ff : 2 * ff]
        down[:, 0, :] = total[:, 2 * ff :]

    came = pl.BlockSpec((tall, 3 * ff), lambda i: (0, 0))
    part = pl.BlockSpec((tall, 1, ff), lambda i: (0, 0, 0))
    return call(
        body,
        (1,),
        [came, came, pl.BlockSpec((1, tall, 3 * ff), lambda i: (at, 0, 0))],
        [part] * 3,
        [jax.ShapeDtypeStruct((tall, 1, ff), F32)] * 3,
        12 * tall * ff,
        36 * tall * ff,
    )(ahead, behind, in_hbm(terms))


def to_tokens(names, came_back):
    held, slots = names.shape
    width = came_back.shape[1]
    wide = 512

    def body(which, back, out):
        out[...] = dot(which[...], back[...], ROW_BY_ROW).astype(BF16)

    return call(
        body,
        (width // wide,),
        [
            pl.BlockSpec((held, slots), lambda j: (0, 0)),
            pl.BlockSpec((slots, wide), lambda j: (0, j)),
        ],
        pl.BlockSpec((held, wide), lambda j: (0, j)),
        shape(held, width, BF16),
        2 * held * slots * width,
        2 * (held + slots) * width,
    )(names, came_back)


def on_device(
    tokens, target, route_index, route_count, route_gate, gate_weight, up_weight, down_weight
):
    groups = lax.axis_size("dp")
    sources = lax.axis_size("expert")
    chips = groups // 2
    local_index = route_index[0, :, 0, :]
    live_count = route_count[0, :, 0]
    per_source = local_index.shape[1]
    held, width = tokens.shape
    tall = gate_weight.shape[0]
    ff = gate_weight.shape[2]
    slots = sources * per_source

    def along(array, by):
        pairs = [
            (2 * z + c, 2 * ((z + by) % chips) + c) for z in range(chips) for c in range(2)
        ]
        return lax.ppermute(array, "dp", pairs)

    def other_core(array):
        return lax.ppermute(array, "dp", [(d, d ^ 1) for d in range(groups)])

    with jax.named_scope("gather_weights"):
        own = side_by_side(gate_weight[:, 0], up_weight[:, 0], down_weight[:, 0])
        full = lax.all_gather(own, "dp", axis=0, tiled=True)

    with jax.named_scope("routing"):
        usable = jnp.arange(per_source, dtype=jnp.int32)[None, :] < live_count[:, None]
        flat_index = local_index.reshape(slots)
        live = usable.reshape(slots)
        weight = jnp.where(live, route_gate[0, :, 0, :].reshape(slots), 0.0)
        names = flat_index[:, None] == jnp.arange(held, dtype=jnp.int32)[None, :]
        pick = (names & live[:, None]).astype(BF16)
        same = flat_index[:, None] == flat_index[None, :]
        high = lax.reduce_precision(weight, 8, 7)
        low = weight - high
        mix_high = jnp.where(same, high[None, :], 0.0).astype(BF16)
        mix_low = jnp.where(same, low[None, :], 0.0).astype(BF16)

    with jax.named_scope("rows_out"):
        rows = dot(pick, tokens, ROW_BY_ROW).astype(BF16)
        expert_rows = exchange(rows.reshape(sources, per_source, width)).reshape(slots, width)
        other_rows = other_core(expert_rows)
        wanted = dot(pick, target, ROW_BY_ROW).astype(BF16)

    with jax.named_scope("forward"):
        gate_pre, up_pre, hidden = project_in(expert_rows, full, ff)
        expert_out = project_out(hidden, full, ff)
        other_hidden = other_core(hidden)

    with jax.named_scope("combine"):
        returned = exchange(expert_out.reshape(sources, per_source, width)).reshape(slots, width)
        slot_grad = combine(mix_high, mix_low, weight[:, None], returned, wanted)
        owner_grad = exchange(slot_grad.reshape(sources, per_source, width)).reshape(slots, width)
        other_grad = other_core(owner_grad)

    with jax.named_scope("backward"):
        pre_grad = back_in(owner_grad, full, gate_pre, up_pre, ff)
        other_pre = other_core(pre_grad)

    with jax.named_scope("weight_gradients"):
        place = lax.axis_index("dp")
        z, core = place // 2, place % 2
        mine = (expert_rows, pre_grad, owner_grad, hidden)
        theirs = (other_rows, other_pre, other_grad, other_hidden)
        far = chips // 2
        steps = [s for near in range(far - 1, 0, -1) for s in (near, chips - near)] + [0]
        blocks = ((z + jnp.array([far] + steps, jnp.int32)) & (chips - 1)) * 2 + core
        ahead, behind = chip_terms(blocks[:1], mine, theirs, True)
        ahead, behind = along(ahead, 1), along(behind, -1)
        terms = chip_terms(blocks[1:], mine, theirs, False)
        for at in range(0, len(steps) - 1, 2):
            ahead, behind = add_terms(ahead, behind, terms, at)
            ahead, behind = along(ahead, 1), along(behind, -1)
        factor = (groups * sources * per_source) ** (-0.5)
        gradients = last_sum(ahead, behind, terms, len(steps) - 1, ff, factor)

    with jax.named_scope("token_gradient"):
        row_grad = back_out(pre_grad, full, ff)
        came_back = exchange(row_grad.reshape(sources, per_source, width)).reshape(slots, width)
        token_grad = to_tokens(names.T.astype(BF16), came_back)

    return (token_grad, *gradients)


def solution(mesh):
    return jax.shard_map(
        on_device,
        mesh=mesh,
        in_specs=(
            P(("dp", "expert"), None),
            P(("dp", "expert"), None),
            P("dp", None, "expert", None),
            P("dp", None, "expert"),
            P("dp", None, "expert", None),
            P("dp", "expert", None),
            P("dp", "expert", None),
            P("dp", "expert", None),
        ),
        out_specs=(
            P(("dp", "expert"), None),
            P("dp", "expert", None),
            P("dp", "expert", None),
            P("dp", "expert", None),
        ),
        check_vma=False,
    )
```

```python
import jax
import jax.numpy as jnp
from jax import lax
from jax.experimental import pallas as pl
from jax.experimental.pallas import tpu as pltpu
from jax.sharding import PartitionSpec as P

F32 = jnp.float32
BF16 = jnp.bfloat16
ROW_BY_ROW = ((1,), (0,))
OVER_LAST = ((1,), (1,))
OVER_FIRST = ((0,), (0,))
MIB = 1024 * 1024
VMEM_LIMIT = 24 * MIB


def exchange(block):
    return lax.all_to_all(block, "expert", split_axis=0, concat_axis=0, tiled=True)


def dot(a, b, dims):
    return lax.dot_general(a, b, (dims, ((), ())), preferred_element_type=F32)


def in_hbm(array):
    return pltpu.with_memory_space_constraint(array, pltpu.HBM)


def held_in_hbm(dims, dtype):
    return pltpu.HBM(dims, dtype)


def call(body, grid, in_specs, out_specs, out_shape, flops, moved, prefetch=0, scratch=()):
    return pl.pallas_call(
        body,
        grid_spec=pltpu.PrefetchScalarGridSpec(
            num_scalar_prefetch=prefetch,
            grid=grid,
            in_specs=in_specs,
            out_specs=out_specs,
            scratch_shapes=list(scratch),
        ),
        out_shape=out_shape,
        compiler_params=pltpu.CompilerParams(vmem_limit_bytes=VMEM_LIMIT),
        cost_estimate=pl.CostEstimate(flops=flops, bytes_accessed=moved, transcendentals=0),
    )


def side_by_side(gate_weight, up_weight, down_weight):
    tall, ff = gate_weight.shape

    def body(g, u, d, out, done):
        copies = [
            pltpu.make_async_copy(part, out.at[:, pl.ds(i * ff, ff)], done.at[i])
            for i, part in enumerate((g, u, d))
        ]
        for copy in copies:
            copy.start()
        for copy in copies:
            copy.wait()

    place = pl.BlockSpec(memory_space=pltpu.HBM)
    return pl.pallas_call(
        body,
        in_specs=[place] * 3,
        out_specs=place,
        out_shape=shape(tall, 3 * ff, BF16),
        scratch_shapes=[pltpu.SemaphoreType.DMA((3,))],
        compiler_params=pltpu.CompilerParams(vmem_limit_bytes=VMEM_LIMIT),
        cost_estimate=pl.CostEstimate(flops=0, bytes_accessed=12 * tall * ff, transcendentals=0),
    )(gate_weight, up_weight, down_weight)


def shape(rows, columns, dtype):
    return jax.ShapeDtypeStruct((rows, columns), dtype)


def add_up(total, step, term):
    @pl.when(step == 0)
    def _():
        total[...] = term

    @pl.when(step > 0)
    def _():
        total[...] += term


def project_in(rows, full, ff):
    slots, width = rows.shape
    tall = 1024
    steps = width // tall

    def body(x, w, pre, hidden, total):
        step = pl.program_id(0)
        add_up(total, step, dot(x[...], w[...], ROW_BY_ROW))

        @pl.when(step == steps - 1)
        def _():
            g, u = total[:, :ff], total[:, ff:]
            pre[...] = total[...]
            hidden[...] = (g * jax.nn.sigmoid(g) * u).astype(BF16)

    return call(
        body,
        (steps,),
        [
            pl.BlockSpec((slots, tall), lambda j: (0, j)),
            pl.BlockSpec((tall, 2 * ff), lambda j: (j, 0)),
        ],
        [pl.BlockSpec((slots, 2 * ff), lambda j: (0, 0)), pl.BlockSpec((slots, ff), lambda j: (0, 0))],
        [shape(slots, 2 * ff, F32), shape(slots, ff, BF16)],
        4 * slots * width * ff,
        4 * width * ff + 2 * slots * width + 10 * slots * ff,
        scratch=[pltpu.VMEM((slots, 2 * ff), F32)],
    )(in_hbm(rows), in_hbm(full))


def project_out(hidden, full, ff):
    slots, width = hidden.shape[0], full.shape[0]
    tall = 1024

    def body(h, wd, out):
        out[...] = dot(h[...], wd[...], OVER_LAST).astype(BF16)

    return call(
        body,
        (width // tall,),
        [
            pl.BlockSpec((slots, ff), lambda j: (0, 0)),
            pl.BlockSpec((tall, ff), lambda j: (j, 2)),
        ],
        pl.BlockSpec((slots, tall), lambda j: (0, j)),
        held_in_hbm((slots, width), BF16),
        2 * slots * width * ff,
        2 * width * ff + 2 * slots * (width + ff),
    )(hidden, in_hbm(full))


def combine(mix_high, mix_low, weight, returned, wanted):
    slots, width = returned.shape
    wide = width

    def body(high, low, w, back, goal, out):
        x = back[...]
        total = dot(high[...], x, ROW_BY_ROW) + dot(low[...], x, ROW_BY_ROW)
        out[...] = (w[...] * (total - goal[...].astype(F32))).astype(BF16)

    mix = pl.BlockSpec((slots, slots), lambda j: (0, 0))
    part = pl.BlockSpec((slots, wide), lambda j: (0, j))
    return call(
        body,
        (width // wide,),
        [mix, mix, pl.BlockSpec((slots, 1), lambda j: (0, 0)), part, part],
        part,
        held_in_hbm((slots, width), BF16),
        4 * slots * slots * width,
        6 * slots * width,
    )(in_hbm(mix_high), in_hbm(mix_low), in_hbm(weight), in_hbm(returned), in_hbm(wanted))


def back_in(owner_grad, full, pre, ff):
    slots, width = owner_grad.shape
    tall = 1024
    steps = width // tall

    def body(x, w, pre_ref, out, total):
        step = pl.program_id(0)
        add_up(total, step, dot(x[...], w[...], ROW_BY_ROW))

        @pl.when(step == steps - 1)
        def _():
            h, g = total[...], pre_ref[:, :ff]
            sig = jax.nn.sigmoid(g)
            out[0] = (h * pre_ref[:, ff:] * sig * (1.0 + g * (1.0 - sig))).astype(BF16)
            out[1] = (h * (g * sig)).astype(BF16)

    return call(
        body,
        (steps,),
        [
            pl.BlockSpec((slots, tall), lambda j: (0, j)),
            pl.BlockSpec((tall, ff), lambda j: (j, 2)),
            pl.BlockSpec((slots, 2 * ff), lambda j: (0, 0)),
        ],
        pl.BlockSpec((2, slots, ff), lambda j: (0, 0, 0)),
        jax.ShapeDtypeStruct((2, slots, ff), BF16),
        2 * slots * width * ff,
        2 * width * ff + 2 * slots * width + 12 * slots * ff,
        scratch=[pltpu.VMEM((slots, ff), F32)],
    )(in_hbm(owner_grad), in_hbm(full), in_hbm(pre))


def back_out(pre_grad, full, ff):
    slots, width = pre_grad.shape[1], full.shape[0]
    tall = 1024

    def body(x, wg, wu, out):
        out[...] = (
            dot(x[0], wg[...], OVER_LAST) + dot(x[1], wu[...], OVER_LAST)
        ).astype(BF16)

    return call(
        body,
        (width // tall,),
        [
            pl.BlockSpec((2, slots, ff), lambda j: (0, 0, 0)),
            pl.BlockSpec((tall, ff), lambda j: (j, 0)),
            pl.BlockSpec((tall, ff), lambda j: (j, 1)),
        ],
        pl.BlockSpec((slots, tall), lambda j: (0, j)),
        held_in_hbm((slots, width), BF16),
        4 * slots * width * ff,
        4 * width * ff + 2 * slots * (width + 2 * ff),
    )(pre_grad, in_hbm(full), in_hbm(full))


def chip_terms(blocks, own, other, halves):
    count = blocks.shape[0]
    slots, ff = own[3].shape
    tall = 128
    rows = tall // 2 if halves else tall
    dtype = BF16 if halves else F32

    def body(names, *refs):
        columns, outs = refs[: 4 * count], refs[4 * count + 4 :]
        pre_own, hidden_own, pre_other, hidden_other = refs[4 * count : 4 * count + 4]
        xa, oa, xb, ob = (
            jnp.concatenate([r[...] for r in columns[i * count : (i + 1) * count]], axis=1)
            for i in range(4)
        )
        gate = dot(xa, pre_own[0], OVER_FIRST) + dot(xb, pre_other[0], OVER_FIRST)
        up = dot(xa, pre_own[1], OVER_FIRST) + dot(xb, pre_other[1], OVER_FIRST)
        down = dot(oa, hidden_own[...], OVER_FIRST) + dot(ob, hidden_other[...], OVER_FIRST)
        for at, part in ((0, gate), (ff, up), (2 * ff, down)):
            for i, out in enumerate(outs):
                out[:, at : at + ff] = part[i * rows : (i + 1) * rows].astype(dtype)

    columns = [pl.BlockSpec((slots, tall), lambda i, names, k=k: (0, names[k])) for k in range(count)]
    pair = pl.BlockSpec((2, slots, ff), lambda i, names: (0, 0, 0))
    whole = pl.BlockSpec((slots, ff), lambda i, names: (0, 0))
    number = 2 if halves else count
    sums = pl.BlockSpec((rows, 3 * ff), lambda i, names: (0, 0))
    return call(
        body,
        (1,),
        columns * 4 + [pair, whole] * 2,
        [sums] * number,
        [shape(rows, 3 * ff, dtype)] * number,
        12 * count * slots * tall * ff,
        12 * slots * ff + count * (8 * slots * tall + 12 * tall * ff),
        prefetch=1,
    )(
        blocks,
        *[array for side in (own, other) for array in (side[0], side[2]) for _ in range(count)],
        *(own[1], own[3], other[1], other[3]),
    )


def add_term(came, term, last_rows=False):
    tall, width = term.shape
    part = came.shape[0]
    first = tall - part if last_rows else 0

    def body(a, mine, out):
        if part < tall:
            out[...] = mine[...].astype(BF16)
        out[first : first + part] = (mine[first : first + part] + a[...].astype(F32)).astype(BF16)

    return call(
        body,
        (1,),
        [
            pl.BlockSpec((part, width), lambda i: (0, 0)),
            pl.BlockSpec((tall, width), lambda i: (0, 0)),
        ],
        pl.BlockSpec((tall, width), lambda i: (0, 0)),
        shape(tall, width, BF16),
        tall * width,
        8 * tall * width,
    )(came, term)


def last_sum(ahead, behind, term, ff, factor):
    tall = ahead.shape[0]

    def body(a, b, mine, gate, up, down):
        total = (a[...].astype(F32) + b[...].astype(F32) + mine[...]) * factor
        gate[:, 0, :] = total[:, :ff]
        up[:, 0, :] = total[:, ff : 2 * ff]
        down[:, 0, :] = total[:, 2 * ff :]

    came = pl.BlockSpec((tall, 3 * ff), lambda i: (0, 0))
    part = pl.BlockSpec((tall, 1, ff), lambda i: (0, 0, 0))
    return call(
        body,
        (1,),
        [came] * 3,
        [part] * 3,
        [jax.ShapeDtypeStruct((tall, 1, ff), F32)] * 3,
        12 * tall * ff,
        36 * tall * ff,
    )(ahead, behind, term)


def to_tokens(names, came_back):
    held, slots = names.shape
    width = came_back.shape[1]
    wide = 1024

    def body(which, back, out):
        out[...] = dot(which[...], back[...], ROW_BY_ROW).astype(BF16)

    return call(
        body,
        (width // wide,),
        [
            pl.BlockSpec((held, slots), lambda j: (0, 0)),
            pl.BlockSpec((slots, wide), lambda j: (0, j)),
        ],
        pl.BlockSpec((held, wide), lambda j: (0, j)),
        shape(held, width, BF16),
        2 * held * slots * width,
        2 * (held + slots) * width,
    )(names, came_back)


def on_device(
    tokens, target, route_index, route_count, route_gate, gate_weight, up_weight, down_weight
):
    groups = lax.axis_size("dp")
    sources = lax.axis_size("expert")
    chips = groups // 2
    local_index = route_index[0, :, 0, :]
    live_count = route_count[0, :, 0]
    per_source = local_index.shape[1]
    held, width = tokens.shape
    tall = gate_weight.shape[0]
    ff = gate_weight.shape[2]
    slots = sources * per_source

    def along(array, by):
        pairs = [
            (2 * z + c, 2 * ((z + by) % chips) + c) for z in range(chips) for c in range(2)
        ]
        return lax.ppermute(array, "dp", pairs)

    def other_core(array):
        return lax.ppermute(array, "dp", [(d, d ^ 1) for d in range(groups)])

    with jax.named_scope("gather_weights"):
        own = side_by_side(gate_weight[:, 0], up_weight[:, 0], down_weight[:, 0])
        full = lax.all_gather(own, "dp", axis=0, tiled=True)

    with jax.named_scope("routing"):
        usable = jnp.arange(per_source, dtype=jnp.int32)[None, :] < live_count[:, None]
        flat_index = local_index.reshape(slots)
        live = usable.reshape(slots)
        weight = jnp.where(live, route_gate[0, :, 0, :].reshape(slots), 0.0)
        names = flat_index[:, None] == jnp.arange(held, dtype=jnp.int32)[None, :]
        pick = (names & live[:, None]).astype(BF16)
        same = flat_index[:, None] == flat_index[None, :]
        high = lax.reduce_precision(weight, 8, 7)
        low = weight - high
        mix_high = jnp.where(same, high[None, :], 0.0).astype(BF16)
        mix_low = jnp.where(same, low[None, :], 0.0).astype(BF16)

    with jax.named_scope("rows_out"):
        rows = dot(pick, tokens, ROW_BY_ROW).astype(BF16)
        expert_rows = exchange(rows.reshape(sources, per_source, width)).reshape(slots, width)
        other_rows = other_core(expert_rows)
        wanted = dot(pick, target, ROW_BY_ROW).astype(BF16)

    with jax.named_scope("forward"):
        pre, hidden = project_in(expert_rows, full, ff)
        expert_out = project_out(hidden, full, ff)
        other_hidden = other_core(hidden)

    with jax.named_scope("combine"):
        returned = exchange(expert_out.reshape(sources, per_source, width)).reshape(slots, width)
        slot_grad = combine(mix_high, mix_low, weight[:, None], returned, wanted)
        owner_grad = exchange(slot_grad.reshape(sources, per_source, width)).reshape(slots, width)
        other_grad = other_core(owner_grad)

    with jax.named_scope("backward"):
        pre_grad = back_in(owner_grad, full, pre, ff)
        other_pre = other_core(pre_grad)

    with jax.named_scope("weight_gradients"):
        place = lax.axis_index("dp")
        z, core = place // 2, place % 2
        mine = (expert_rows, pre_grad, owner_grad, hidden)
        theirs = (other_rows, other_pre, other_grad, other_hidden)
        far = chips // 2
        place_of = lambda steps: (((z + jnp.array(steps, jnp.int32)) & (chips - 1)) * 2 + core)
        ahead, behind = chip_terms(place_of([far]), mine, theirs, True)
        ahead, behind = along(ahead, 1), along(behind, -1)
        for near in range(far - 1, 0, -1):
            first, second = chip_terms(place_of([near, chips - near]), mine, theirs, False)
            ahead, behind = add_term(ahead, first), add_term(behind, second, True)
            ahead, behind = along(ahead, 1), along(behind, -1)
        factor = (groups * sources * per_source) ** (-0.5)
        (term,) = chip_terms(place_of([0]), mine, theirs, False)
        gradients = last_sum(ahead, behind, term, ff, factor)

    with jax.named_scope("token_gradient"):
        row_grad = back_out(pre_grad, full, ff)
        came_back = exchange(row_grad.reshape(sources, per_source, width)).reshape(slots, width)
        token_grad = to_tokens(names.T.astype(BF16), came_back)

    return (token_grad, *gradients)


def solution(mesh):
    return jax.shard_map(
        on_device,
        mesh=mesh,
        in_specs=(
            P(("dp", "expert"), None),
            P(("dp", "expert"), None),
            P("dp", None, "expert", None),
            P("dp", None, "expert"),
            P("dp", None, "expert", None),
            P("dp", "expert", None),
            P("dp", "expert", None),
            P("dp", "expert", None),
        ),
        out_specs=(
            P(("dp", "expert"), None),
            P("dp", "expert", None),
            P("dp", "expert", None),
            P("dp", "expert", None),
        ),
        check_vma=False,
    )
```

```python
import jax
import jax.numpy as jnp
from jax import lax
from jax.experimental import pallas as pl
from jax.experimental.pallas import tpu as pltpu
from jax.sharding import PartitionSpec as P

F32 = jnp.float32
BF16 = jnp.bfloat16
ROW_BY_ROW = ((1,), (0,))
OVER_LAST = ((1,), (1,))
OVER_FIRST = ((0,), (0,))
MIB = 1024 * 1024
VMEM_LIMIT = 24 * MIB


def exchange(block):
    return lax.all_to_all(block, "expert", split_axis=0, concat_axis=0, tiled=True)


def dot(a, b, dims):
    return lax.dot_general(a, b, (dims, ((), ())), preferred_element_type=F32)


def in_hbm(array):
    return pltpu.with_memory_space_constraint(array, pltpu.HBM)


UNREAD = pl.BlockSpec(memory_space=pltpu.HBM)


def held_in_hbm(dims, dtype):
    return pltpu.HBM(dims, dtype)


def call(body, grid, in_specs, out_specs, out_shape, flops, moved, prefetch=0, scratch=()):
    return pl.pallas_call(
        body,
        grid_spec=pltpu.PrefetchScalarGridSpec(
            num_scalar_prefetch=prefetch,
            grid=grid,
            in_specs=in_specs,
            out_specs=out_specs,
            scratch_shapes=list(scratch),
        ),
        out_shape=out_shape,
        compiler_params=pltpu.CompilerParams(vmem_limit_bytes=VMEM_LIMIT),
        cost_estimate=pl.CostEstimate(flops=flops, bytes_accessed=moved, transcendentals=0),
    )


def side_by_side(gate_weight, up_weight, down_weight):
    tall, ff = gate_weight.shape

    def body(g, u, d, out):
        out[:, :ff] = g[...]
        out[:, ff : 2 * ff] = u[...]
        out[:, 2 * ff :] = d[...]

    part = pl.BlockSpec((tall, ff), lambda i: (0, 0))
    return call(
        body,
        (1,),
        [part] * 3,
        pl.BlockSpec((tall, 3 * ff), lambda i: (0, 0)),
        held_in_hbm((tall, 3 * ff), BF16),
        0,
        12 * tall * ff,
    )(in_hbm(gate_weight), in_hbm(up_weight), in_hbm(down_weight))


def shape(rows, columns, dtype):
    return jax.ShapeDtypeStruct((rows, columns), dtype)


def add_up(total, step, term):
    @pl.when(step == 0)
    def _():
        total[...] = term

    @pl.when(step > 0)
    def _():
        total[...] += term


def project_in(rows, full, ff, after):
    slots, width = rows.shape
    tall = 1024
    steps = width // tall

    def body(x, w, _, pre, hidden, total):
        step = pl.program_id(0)
        add_up(total, step, dot(x[...], w[...], ROW_BY_ROW))

        @pl.when(step == steps - 1)
        def _():
            g, u = total[:, :ff], total[:, ff:]
            pre[...] = total[...]
            hidden[...] = (g * jax.nn.sigmoid(g) * u).astype(BF16)

    return call(
        body,
        (steps,),
        [
            pl.BlockSpec((slots, tall), lambda j: (0, j)),
            pl.BlockSpec((tall, 2 * ff), lambda j: (j, 0)),
            UNREAD,
        ],
        [pl.BlockSpec((slots, 2 * ff), lambda j: (0, 0)), pl.BlockSpec((slots, ff), lambda j: (0, 0))],
        [shape(slots, 2 * ff, F32), shape(slots, ff, BF16)],
        4 * slots * width * ff,
        4 * width * ff + 2 * slots * width + 10 * slots * ff,
        scratch=[pltpu.VMEM((slots, 2 * ff), F32)],
    )(in_hbm(rows), in_hbm(full), in_hbm(after))


def project_out(hidden, full, ff):
    slots, width = hidden.shape[0], full.shape[0]
    tall = 1024

    def body(h, wd, out):
        out[...] = dot(h[...], wd[...], OVER_LAST).astype(BF16)

    return call(
        body,
        (width // tall,),
        [
            pl.BlockSpec((slots, ff), lambda j: (0, 0)),
            pl.BlockSpec((tall, ff), lambda j: (j, 2)),
        ],
        pl.BlockSpec((slots, tall), lambda j: (0, j)),
        held_in_hbm((slots, width), BF16),
        2 * slots * width * ff,
        2 * width * ff + 2 * slots * (width + ff),
    )(hidden, in_hbm(full))


def combine(mix_high, mix_low, weight, returned, wanted, after):
    slots, width = returned.shape
    wide = width

    def body(high, low, w, back, goal, _, out):
        x = back[...]
        total = dot(high[...], x, ROW_BY_ROW) + dot(low[...], x, ROW_BY_ROW)
        out[...] = (w[...] * (total - goal[...].astype(F32))).astype(BF16)

    mix = pl.BlockSpec((slots, slots), lambda j: (0, 0))
    part = pl.BlockSpec((slots, wide), lambda j: (0, j))
    return call(
        body,
        (width // wide,),
        [mix, mix, pl.BlockSpec((slots, 1), lambda j: (0, 0)), part, part, UNREAD],
        part,
        held_in_hbm((slots, width), BF16),
        4 * slots * slots * width,
        6 * slots * width,
    )(in_hbm(mix_high), in_hbm(mix_low), in_hbm(weight), in_hbm(returned), in_hbm(wanted), in_hbm(after))


def back_in(owner_grad, full, pre, ff):
    slots, width = owner_grad.shape
    tall = 1024
    steps = width // tall

    def body(x, w, pre_ref, out, total):
        step = pl.program_id(0)
        add_up(total, step, dot(x[...], w[...], ROW_BY_ROW))

        @pl.when(step == steps - 1)
        def _():
            h, g = total[...], pre_ref[:, :ff]
            sig = jax.nn.sigmoid(g)
            out[0] = (h * pre_ref[:, ff:] * sig * (1.0 + g * (1.0 - sig))).astype(BF16)
            out[1] = (h * (g * sig)).astype(BF16)

    return call(
        body,
        (steps,),
        [
            pl.BlockSpec((slots, tall), lambda j: (0, j)),
            pl.BlockSpec((tall, ff), lambda j: (j, 2)),
            pl.BlockSpec((slots, 2 * ff), lambda j: (0, 0)),
        ],
        pl.BlockSpec((2, slots, ff), lambda j: (0, 0, 0)),
        jax.ShapeDtypeStruct((2, slots, ff), BF16),
        2 * slots * width * ff,
        2 * width * ff + 2 * slots * width + 12 * slots * ff,
        scratch=[pltpu.VMEM((slots, ff), F32)],
    )(in_hbm(owner_grad), in_hbm(full), in_hbm(pre))


def back_out(pre_grad, full, ff):
    slots, width = pre_grad.shape[1], full.shape[0]
    tall = 1024

    def body(x, wg, wu, out):
        out[...] = (
            dot(x[0], wg[...], OVER_LAST) + dot(x[1], wu[...], OVER_LAST)
        ).astype(BF16)

    return call(
        body,
        (width // tall,),
        [
            pl.BlockSpec((2, slots, ff), lambda j: (0, 0, 0)),
            pl.BlockSpec((tall, ff), lambda j: (j, 0)),
            pl.BlockSpec((tall, ff), lambda j: (j, 1)),
        ],
        pl.BlockSpec((slots, tall), lambda j: (0, j)),
        held_in_hbm((slots, width), BF16),
        4 * slots * width * ff,
        4 * width * ff + 2 * slots * (width + 2 * ff),
    )(pre_grad, in_hbm(full), in_hbm(full))


def chip_terms(blocks, own, other, halves):
    count = blocks.shape[0]
    slots, ff = own[3].shape
    tall = 128
    rows = tall // 2 if halves else tall
    dtype = BF16 if halves else F32

    def body(names, *refs):
        columns, outs = refs[: 4 * count], refs[4 * count + 4 :]
        pre_own, hidden_own, pre_other, hidden_other = refs[4 * count : 4 * count + 4]
        xa, oa, xb, ob = (
            jnp.concatenate([r[...] for r in columns[i * count : (i + 1) * count]], axis=1)
            for i in range(4)
        )
        gate = dot(xa, pre_own[0], OVER_FIRST) + dot(xb, pre_other[0], OVER_FIRST)
        up = dot(xa, pre_own[1], OVER_FIRST) + dot(xb, pre_other[1], OVER_FIRST)
        down = dot(oa, hidden_own[...], OVER_FIRST) + dot(ob, hidden_other[...], OVER_FIRST)
        for at, part in ((0, gate), (ff, up), (2 * ff, down)):
            for i, out in enumerate(outs):
                out[:, at : at + ff] = part[i * rows : (i + 1) * rows].astype(dtype)

    columns = [pl.BlockSpec((slots, tall), lambda i, names, k=k: (0, names[k])) for k in range(count)]
    pair = pl.BlockSpec((2, slots, ff), lambda i, names: (0, 0, 0))
    whole = pl.BlockSpec((slots, ff), lambda i, names: (0, 0))
    number = 2 if halves else count
    sums = pl.BlockSpec((rows, 3 * ff), lambda i, names: (0, 0))
    return call(
        body,
        (1,),
        columns * 4 + [pair, whole] * 2,
        [sums] * number,
        [shape(rows, 3 * ff, dtype)] * number,
        12 * count * slots * tall * ff,
        12 * slots * ff + count * (8 * slots * tall + 12 * tall * ff),
        prefetch=1,
    )(
        blocks,
        *[array for side in (own, other) for array in (side[0], side[2]) for _ in range(count)],
        *(own[1], own[3], other[1], other[3]),
    )


def add_term(came, term, last_rows=False, after=()):
    tall, width = term.shape
    part = came.shape[0]
    first = tall - part if last_rows else 0

    def body(a, mine, *refs):
        out = refs[-1]
        if part < tall:
            out[...] = mine[...].astype(BF16)
        out[first : first + part] = (mine[first : first + part] + a[...].astype(F32)).astype(BF16)

    return call(
        body,
        (1,),
        [
            pl.BlockSpec((part, width), lambda i: (0, 0)),
            pl.BlockSpec((tall, width), lambda i: (0, 0)),
        ]
        + [UNREAD] * len(after),
        pl.BlockSpec((tall, width), lambda i: (0, 0)),
        shape(tall, width, BF16),
        tall * width,
        8 * tall * width,
    )(came, term, *map(in_hbm, after))


def last_sum(ahead, behind, term, ff, factor):
    tall = ahead.shape[0]

    def body(a, b, mine, gate, up, down):
        total = (a[...].astype(F32) + b[...].astype(F32) + mine[...]) * factor
        gate[:, 0, :] = total[:, :ff]
        up[:, 0, :] = total[:, ff : 2 * ff]
        down[:, 0, :] = total[:, 2 * ff :]

    came = pl.BlockSpec((tall, 3 * ff), lambda i: (0, 0))
    part = pl.BlockSpec((tall, 1, ff), lambda i: (0, 0, 0))
    return call(
        body,
        (1,),
        [came] * 3,
        [part] * 3,
        [jax.ShapeDtypeStruct((tall, 1, ff), F32)] * 3,
        12 * tall * ff,
        36 * tall * ff,
    )(ahead, behind, term)


def to_tokens(names, came_back):
    held, slots = names.shape
    width = came_back.shape[1]
    wide = 1024

    def body(which, back, out):
        out[...] = dot(which[...], back[...], ROW_BY_ROW).astype(BF16)

    return call(
        body,
        (width // wide,),
        [
            pl.BlockSpec((held, slots), lambda j: (0, 0)),
            pl.BlockSpec((slots, wide), lambda j: (0, j)),
        ],
        pl.BlockSpec((held, wide), lambda j: (0, j)),
        shape(held, width, BF16),
        2 * held * slots * width,
        2 * (held + slots) * width,
    )(names, came_back)


def on_device(
    tokens, target, route_index, route_count, route_gate, gate_weight, up_weight, down_weight
):
    groups = lax.axis_size("dp")
    sources = lax.axis_size("expert")
    chips = groups // 2
    local_index = route_index[0, :, 0, :]
    live_count = route_count[0, :, 0]
    per_source = local_index.shape[1]
    held, width = tokens.shape
    tall = gate_weight.shape[0]
    ff = gate_weight.shape[2]
    slots = sources * per_source

    def along(array, by):
        pairs = [
            (2 * z + c, 2 * ((z + by) % chips) + c) for z in range(chips) for c in range(2)
        ]
        return lax.ppermute(array, "dp", pairs)

    def other_core(array):
        return lax.ppermute(array, "dp", [(d, d ^ 1) for d in range(groups)])

    with jax.named_scope("gather_weights"):
        own = side_by_side(gate_weight[:, 0], up_weight[:, 0], down_weight[:, 0])
        full = lax.all_gather(own, "dp", axis=0, tiled=True)

    with jax.named_scope("routing"):
        usable = jnp.arange(per_source, dtype=jnp.int32)[None, :] < live_count[:, None]
        flat_index = local_index.reshape(slots)
        live = usable.reshape(slots)
        weight = jnp.where(live, route_gate[0, :, 0, :].reshape(slots), 0.0)
        names = flat_index[:, None] == jnp.arange(held, dtype=jnp.int32)[None, :]
        pick = (names & live[:, None]).astype(BF16)
        same = flat_index[:, None] == flat_index[None, :]
        high = lax.reduce_precision(weight, 8, 7)
        low = weight - high
        mix_high = jnp.where(same, high[None, :], 0.0).astype(BF16)
        mix_low = jnp.where(same, low[None, :], 0.0).astype(BF16)

    with jax.named_scope("rows_out"):
        rows = dot(pick, tokens, ROW_BY_ROW).astype(BF16)
        expert_rows = exchange(rows.reshape(sources, per_source, width)).reshape(slots, width)
        other_rows = other_core(expert_rows)
        wanted = dot(pick, target, ROW_BY_ROW).astype(BF16)

    with jax.named_scope("forward"):
        pre, hidden = project_in(expert_rows, full, ff, other_rows)
        expert_out = project_out(hidden, full, ff)
        other_hidden = other_core(hidden)

    with jax.named_scope("combine"):
        returned = exchange(expert_out.reshape(sources, per_source, width)).reshape(slots, width)
        slot_grad = combine(
            mix_high, mix_low, weight[:, None], returned, wanted, other_hidden
        )
        owner_grad = exchange(slot_grad.reshape(sources, per_source, width)).reshape(slots, width)
        other_grad = other_core(owner_grad)

    with jax.named_scope("backward"):
        pre_grad = back_in(owner_grad, full, pre, ff)
        other_pre = other_core(pre_grad)
        row_grad = back_out(pre_grad, full, ff)

    with jax.named_scope("weight_gradients"):
        place = lax.axis_index("dp")
        z, core = place // 2, place % 2
        mine = (expert_rows, pre_grad, owner_grad, hidden)
        theirs = (other_rows, other_pre, other_grad, other_hidden)
        far = chips // 2
        place_of = lambda steps: (((z + jnp.array(steps, jnp.int32)) & (chips - 1)) * 2 + core)
        ahead, behind = chip_terms(place_of([far]), mine, theirs, True)
        ahead, behind = along(ahead, 1), along(behind, -1)
        for near in range(far - 1, 0, -1):
            first, second = chip_terms(place_of([near, chips - near]), mine, theirs, False)
            after = (row_grad,) if near == far - 2 else ()
            ahead, behind = add_term(ahead, first, False, after), add_term(behind, second, True, after)
            ahead, behind = along(ahead, 1), along(behind, -1)
        factor = (groups * sources * per_source) ** (-0.5)
        (term,) = chip_terms(place_of([0]), mine, theirs, False)
        gradients = last_sum(ahead, behind, term, ff, factor)

    with jax.named_scope("token_gradient"):
        came_back = exchange(row_grad.reshape(sources, per_source, width)).reshape(slots, width)
        token_grad = to_tokens(names.T.astype(BF16), came_back)

    return (token_grad, *gradients)


def solution(mesh):
    return jax.shard_map(
        on_device,
        mesh=mesh,
        in_specs=(
            P(("dp", "expert"), None),
            P(("dp", "expert"), None),
            P("dp", None, "expert", None),
            P("dp", None, "expert"),
            P("dp", None, "expert", None),
            P("dp", "expert", None),
            P("dp", "expert", None),
            P("dp", "expert", None),
        ),
        out_specs=(
            P(("dp", "expert"), None),
            P("dp", "expert", None),
            P("dp", "expert", None),
            P("dp", "expert", None),
        ),
        check_vma=False,
    )
```

```python
import jax
import jax.numpy as jnp
from jax import lax
from jax.experimental import pallas as pl
from jax.experimental.pallas import tpu as pltpu
from jax.sharding import PartitionSpec as P

F32 = jnp.float32
BF16 = jnp.bfloat16
ROW_BY_ROW = ((1,), (0,))
OVER_LAST = ((1,), (1,))
OVER_FIRST = ((0,), (0,))
MIB = 1024 * 1024
VMEM_LIMIT = 24 * MIB


def exchange(block):
    return lax.all_to_all(block, "expert", split_axis=0, concat_axis=0, tiled=True)


def dot(a, b, dims):
    return lax.dot_general(a, b, (dims, ((), ())), preferred_element_type=F32)


def in_hbm(array):
    return pltpu.with_memory_space_constraint(array, pltpu.HBM)


UNREAD = pl.BlockSpec(memory_space=pltpu.HBM)


def held_in_hbm(dims, dtype):
    return pltpu.HBM(dims, dtype)


def call(body, grid, in_specs, out_specs, out_shape, flops, moved, prefetch=0, scratch=()):
    return pl.pallas_call(
        body,
        grid_spec=pltpu.PrefetchScalarGridSpec(
            num_scalar_prefetch=prefetch,
            grid=grid,
            in_specs=in_specs,
            out_specs=out_specs,
            scratch_shapes=list(scratch),
        ),
        out_shape=out_shape,
        compiler_params=pltpu.CompilerParams(vmem_limit_bytes=VMEM_LIMIT),
        cost_estimate=pl.CostEstimate(flops=flops, bytes_accessed=moved, transcendentals=0),
    )


def side_by_side(gate_weight, up_weight, down_weight):
    tall, ff = gate_weight.shape

    def body(g, u, d, out):
        out[:, :ff] = g[...]
        out[:, ff : 2 * ff] = u[...]
        out[:, 2 * ff :] = d[...]

    part = pl.BlockSpec((tall, ff), lambda i: (0, 0))
    return call(
        body,
        (1,),
        [part] * 3,
        pl.BlockSpec((tall, 3 * ff), lambda i: (0, 0)),
        held_in_hbm((tall, 3 * ff), BF16),
        0,
        12 * tall * ff,
    )(in_hbm(gate_weight), in_hbm(up_weight), in_hbm(down_weight))


def shape(rows, columns, dtype):
    return jax.ShapeDtypeStruct((rows, columns), dtype)


def add_up(total, step, term):
    @pl.when(step == 0)
    def _():
        total[...] = term

    @pl.when(step > 0)
    def _():
        total[...] += term


def project_in(rows, full, ff, after):
    slots, width = rows.shape
    tall = 1024
    steps = width // tall

    def body(x, w, _, pre, hidden, total):
        step = pl.program_id(0)
        add_up(total, step, dot(x[...], w[...], ROW_BY_ROW))

        @pl.when(step == steps - 1)
        def _():
            g, u = total[:, :ff], total[:, ff:]
            pre[...] = total[...]
            hidden[...] = (g * jax.nn.sigmoid(g) * u).astype(BF16)

    return call(
        body,
        (steps,),
        [
            pl.BlockSpec((slots, tall), lambda j: (0, j)),
            pl.BlockSpec((tall, 2 * ff), lambda j: (j, 0)),
            UNREAD,
        ],
        [pl.BlockSpec((slots, 2 * ff), lambda j: (0, 0)), pl.BlockSpec((slots, ff), lambda j: (0, 0))],
        [shape(slots, 2 * ff, F32), shape(slots, ff, BF16)],
        4 * slots * width * ff,
        4 * width * ff + 2 * slots * width + 10 * slots * ff,
        scratch=[pltpu.VMEM((slots, 2 * ff), F32)],
    )(in_hbm(rows), in_hbm(full), in_hbm(after))


def project_out(hidden, full, ff):
    slots, width = hidden.shape[0], full.shape[0]
    tall = 1024

    def body(h, wd, out):
        out[...] = dot(h[...], wd[...], OVER_LAST).astype(BF16)

    return call(
        body,
        (width // tall,),
        [
            pl.BlockSpec((slots, ff), lambda j: (0, 0)),
            pl.BlockSpec((tall, ff), lambda j: (j, 2)),
        ],
        pl.BlockSpec((slots, tall), lambda j: (0, j)),
        held_in_hbm((slots, width), BF16),
        2 * slots * width * ff,
        2 * width * ff + 2 * slots * (width + ff),
    )(hidden, in_hbm(full))


def combine(mix_high, mix_low, weight, returned, wanted, after):
    slots, width = returned.shape
    wide = width

    def body(high, low, w, back, goal, _, out):
        x = back[...]
        total = dot(high[...], x, ROW_BY_ROW) + dot(low[...], x, ROW_BY_ROW)
        out[...] = (w[...] * (total - goal[...].astype(F32))).astype(BF16)

    mix = pl.BlockSpec((slots, slots), lambda j: (0, 0))
    part = pl.BlockSpec((slots, wide), lambda j: (0, j))
    return call(
        body,
        (width // wide,),
        [mix, mix, pl.BlockSpec((slots, 1), lambda j: (0, 0)), part, part, UNREAD],
        part,
        held_in_hbm((slots, width), BF16),
        4 * slots * slots * width,
        6 * slots * width,
    )(in_hbm(mix_high), in_hbm(mix_low), in_hbm(weight), in_hbm(returned), in_hbm(wanted), in_hbm(after))


def back_in(owner_grad, full, pre, ff):
    slots, width = owner_grad.shape
    tall = 1024
    steps = width // tall

    def body(x, w, pre_ref, out, total):
        step = pl.program_id(0)
        add_up(total, step, dot(x[...], w[...], ROW_BY_ROW))

        @pl.when(step == steps - 1)
        def _():
            h, g = total[...], pre_ref[:, :ff]
            sig = jax.nn.sigmoid(g)
            out[0] = (h * pre_ref[:, ff:] * sig * (1.0 + g * (1.0 - sig))).astype(BF16)
            out[1] = (h * (g * sig)).astype(BF16)

    return call(
        body,
        (steps,),
        [
            pl.BlockSpec((slots, tall), lambda j: (0, j)),
            pl.BlockSpec((tall, ff), lambda j: (j, 2)),
            pl.BlockSpec((slots, 2 * ff), lambda j: (0, 0)),
        ],
        pl.BlockSpec((2, slots, ff), lambda j: (0, 0, 0)),
        jax.ShapeDtypeStruct((2, slots, ff), BF16),
        2 * slots * width * ff,
        2 * width * ff + 2 * slots * width + 12 * slots * ff,
        scratch=[pltpu.VMEM((slots, ff), F32)],
    )(in_hbm(owner_grad), in_hbm(full), in_hbm(pre))


def back_out(pre_grad, full, ff):
    slots, width = pre_grad.shape[1], full.shape[0]
    tall = 1024

    def body(x, wg, wu, out):
        out[...] = (
            dot(x[0], wg[...], OVER_LAST) + dot(x[1], wu[...], OVER_LAST)
        ).astype(BF16)

    return call(
        body,
        (width // tall,),
        [
            pl.BlockSpec((2, slots, ff), lambda j: (0, 0, 0)),
            pl.BlockSpec((tall, ff), lambda j: (j, 0)),
            pl.BlockSpec((tall, ff), lambda j: (j, 1)),
        ],
        pl.BlockSpec((slots, tall), lambda j: (0, j)),
        held_in_hbm((slots, width), BF16),
        4 * slots * width * ff,
        4 * width * ff + 2 * slots * (width + 2 * ff),
    )(pre_grad, in_hbm(full), in_hbm(full))


def chip_terms(blocks, own, other, halves):
    count = blocks.shape[0]
    slots, ff = own[3].shape
    tall = 128
    rows = tall // 2 if halves else tall
    dtype = BF16 if halves else F32

    def body(names, *refs):
        columns, outs = refs[: 4 * count], refs[4 * count + 4 :]
        pre_own, hidden_own, pre_other, hidden_other = refs[4 * count : 4 * count + 4]
        xa, oa, xb, ob = (
            jnp.concatenate([r[...] for r in columns[i * count : (i + 1) * count]], axis=1)
            for i in range(4)
        )
        gate = dot(xa, pre_own[0], OVER_FIRST) + dot(xb, pre_other[0], OVER_FIRST)
        up = dot(xa, pre_own[1], OVER_FIRST) + dot(xb, pre_other[1], OVER_FIRST)
        down = dot(oa, hidden_own[...], OVER_FIRST) + dot(ob, hidden_other[...], OVER_FIRST)
        for at, part in ((0, gate), (ff, up), (2 * ff, down)):
            for i, out in enumerate(outs):
                out[:, at : at + ff] = part[i * rows : (i + 1) * rows].astype(dtype)

    columns = [pl.BlockSpec((slots, tall), lambda i, names, k=k: (0, names[k])) for k in range(count)]
    pair = pl.BlockSpec((2, slots, ff), lambda i, names: (0, 0, 0))
    whole = pl.BlockSpec((slots, ff), lambda i, names: (0, 0))
    number = 2 if halves else count
    sums = pl.BlockSpec((rows, 3 * ff), lambda i, names: (0, 0))
    return call(
        body,
        (1,),
        columns * 4 + [pair, whole] * 2,
        [sums] * number,
        [shape(rows, 3 * ff, dtype)] * number,
        12 * count * slots * tall * ff,
        12 * slots * ff + count * (8 * slots * tall + 12 * tall * ff),
        prefetch=1,
    )(
        blocks,
        *[array for side in (own, other) for array in (side[0], side[2]) for _ in range(count)],
        *(own[1], own[3], other[1], other[3]),
    )


def add_term(came, term, last_rows=False, after=()):
    tall, width = term.shape
    part = came.shape[0]
    first = tall - part if last_rows else 0

    def body(a, mine, *refs):
        out = refs[-1]
        if part < tall:
            out[...] = mine[...].astype(BF16)
        out[first : first + part] = (mine[first : first + part] + a[...].astype(F32)).astype(BF16)

    return call(
        body,
        (1,),
        [
            pl.BlockSpec((part, width), lambda i: (0, 0)),
            pl.BlockSpec((tall, width), lambda i: (0, 0)),
        ]
        + [UNREAD] * len(after),
        pl.BlockSpec((tall, width), lambda i: (0, 0)),
        pltpu.VMEM((tall, width), BF16),
        tall * width,
        8 * tall * width,
    )(came, term, *map(in_hbm, after))


def last_sum(ahead, behind, term, ff, factor):
    tall = ahead.shape[0]

    def body(a, b, mine, gate, up, down):
        total = (a[...].astype(F32) + b[...].astype(F32) + mine[...]) * factor
        gate[:, 0, :] = total[:, :ff]
        up[:, 0, :] = total[:, ff : 2 * ff]
        down[:, 0, :] = total[:, 2 * ff :]

    came = pl.BlockSpec((tall, 3 * ff), lambda i: (0, 0))
    part = pl.BlockSpec((tall, 1, ff), lambda i: (0, 0, 0))
    return call(
        body,
        (1,),
        [came] * 3,
        [part] * 3,
        [jax.ShapeDtypeStruct((tall, 1, ff), F32)] * 3,
        12 * tall * ff,
        36 * tall * ff,
    )(ahead, behind, term)


def to_tokens(names, came_back):
    held, slots = names.shape
    width = came_back.shape[1]
    wide = 1024

    def body(which, back, out):
        out[...] = dot(which[...], back[...], ROW_BY_ROW).astype(BF16)

    return call(
        body,
        (width // wide,),
        [
            pl.BlockSpec((held, slots), lambda j: (0, 0)),
            pl.BlockSpec((slots, wide), lambda j: (0, j)),
        ],
        pl.BlockSpec((held, wide), lambda j: (0, j)),
        shape(held, width, BF16),
        2 * held * slots * width,
        2 * (held + slots) * width,
    )(in_hbm(names), in_hbm(came_back))


def on_device(
    tokens, target, route_index, route_count, route_gate, gate_weight, up_weight, down_weight
):
    groups = lax.axis_size("dp")
    sources = lax.axis_size("expert")
    chips = groups // 2
    local_index = route_index[0, :, 0, :]
    live_count = route_count[0, :, 0]
    per_source = local_index.shape[1]
    held, width = tokens.shape
    tall = gate_weight.shape[0]
    ff = gate_weight.shape[2]
    slots = sources * per_source

    def along(array, by):
        pairs = [
            (2 * z + c, 2 * ((z + by) % chips) + c) for z in range(chips) for c in range(2)
        ]
        return lax.ppermute(array, "dp", pairs)

    def other_core(array):
        return lax.ppermute(array, "dp", [(d, d ^ 1) for d in range(groups)])

    with jax.named_scope("gather_weights"):
        own = side_by_side(gate_weight[:, 0], up_weight[:, 0], down_weight[:, 0])
        full = lax.all_gather(own, "dp", axis=0, tiled=True)

    with jax.named_scope("routing"):
        usable = jnp.arange(per_source, dtype=jnp.int32)[None, :] < live_count[:, None]
        flat_index = local_index.reshape(slots)
        live = usable.reshape(slots)
        weight = jnp.where(live, route_gate[0, :, 0, :].reshape(slots), 0.0)
        names = flat_index[:, None] == jnp.arange(held, dtype=jnp.int32)[None, :]
        pick = (names & live[:, None]).astype(BF16)
        same = flat_index[:, None] == flat_index[None, :]
        high = lax.reduce_precision(weight, 8, 7)
        low = weight - high
        mix_high = jnp.where(same, high[None, :], 0.0).astype(BF16)
        mix_low = jnp.where(same, low[None, :], 0.0).astype(BF16)

    with jax.named_scope("rows_out"):
        rows = dot(pick, tokens, ROW_BY_ROW).astype(BF16)
        expert_rows = exchange(rows.reshape(sources, per_source, width)).reshape(slots, width)
        other_rows = other_core(expert_rows)
        wanted = dot(pick, target, ROW_BY_ROW).astype(BF16)

    with jax.named_scope("forward"):
        pre, hidden = project_in(expert_rows, full, ff, other_rows)
        expert_out = project_out(hidden, full, ff)
        other_hidden = other_core(hidden)

    with jax.named_scope("combine"):
        returned = exchange(expert_out.reshape(sources, per_source, width)).reshape(slots, width)
        slot_grad = combine(
            mix_high, mix_low, weight[:, None], returned, wanted, other_hidden
        )
        owner_grad = exchange(slot_grad.reshape(sources, per_source, width)).reshape(slots, width)
        other_grad = other_core(owner_grad)

    with jax.named_scope("backward"):
        pre_grad = back_in(owner_grad, full, pre, ff)
        other_pre = other_core(pre_grad)
        row_grad = back_out(pre_grad, full, ff)

    with jax.named_scope("weight_gradients"):
        place = lax.axis_index("dp")
        z, core = place // 2, place % 2
        mine = (expert_rows, pre_grad, owner_grad, hidden)
        theirs = (other_rows, other_pre, other_grad, other_hidden)
        far = chips // 2
        place_of = lambda steps: (((z + jnp.array(steps, jnp.int32)) & (chips - 1)) * 2 + core)
        ahead, behind = chip_terms(place_of([far]), mine, theirs, True)
        ahead, behind = along(ahead, 1), along(behind, -1)
        for near in range(far - 1, 0, -1):
            first, second = chip_terms(place_of([near, chips - near]), mine, theirs, False)
            after = (row_grad,) if near == far - 2 else ()
            ahead, behind = add_term(ahead, first, False, after), add_term(behind, second, True, after)
            ahead, behind = along(ahead, 1), along(behind, -1)
        factor = (groups * sources * per_source) ** (-0.5)
        (term,) = chip_terms(place_of([0]), mine, theirs, False)
        gradients = last_sum(ahead, behind, term, ff, factor)

    with jax.named_scope("token_gradient"):
        came_back = exchange(row_grad.reshape(sources, per_source, width)).reshape(slots, width)
        token_grad = to_tokens(names.T.astype(BF16), came_back)

    return (token_grad, *gradients)


def solution(mesh):
    return jax.shard_map(
        on_device,
        mesh=mesh,
        in_specs=(
            P(("dp", "expert"), None),
            P(("dp", "expert"), None),
            P("dp", None, "expert", None),
            P("dp", None, "expert"),
            P("dp", None, "expert", None),
            P("dp", "expert", None),
            P("dp", "expert", None),
            P("dp", "expert", None),
        ),
        out_specs=(
            P(("dp", "expert"), None),
            P("dp", "expert", None),
            P("dp", "expert", None),
            P("dp", "expert", None),
        ),
        check_vma=False,
    )
```
